512 devices in a mesh: lon: 64 (over y, z_hi, core), lat: 8 (over x, z_lo).
Axes of the slice: x: 4, y: 8, z: 8 (z_hi: 4, z_lo: 2; z = z_hi * 2 + z_lo), core: 2. Of those that a mesh axis runs over, the one named last changes fastest.
Arguments:
- field: bfloat16 [96, 128, 8192], P(None, 'lat', 'lon'), may hold values from -6 to 6
- land_mask: int32 [128, 8192], P('lat', 'lon'), may hold values from 0 to 1, as said below
- depth_kernel: float32 [2, 96, 7, 7], replicated, may hold values from -0.875 to 0.875
- depth_bias: float32 [2, 96], replicated, may hold values from -3 to 3
- norm_gain: float32 [2, 96], replicated, may hold values from 0.1 to 1.9
- norm_bias: float32 [2, 96], replicated, may hold values from -3 to 3
- w_expand: bfloat16 [2, 384, 96], replicated, may hold values from -0.625 to 0.625
- b_expand: float32 [2, 384], replicated, may hold values from -3 to 3
- w_reduce: bfloat16 [2, 96, 384], replicated, may hold values from -0.3125 to 0.3125
- b_reduce: float32 [2, 96], replicated, may hold values from -3 to 3
Outputs:
- output_field: bfloat16 [96, 128, 8192], P(None, 'lat', 'lon')
The draws below stay inside these ranges and needn't reach their ends.
Inputs may be any that keep to these rules, and one draw needn't show every extreme that they name: `land_mask`: land and ocean come in regions; some aligned blocks of 8 rows and 128 columns are all land.
All inputs are finite; a program needn't handle non-finite values.
Results may differ from the reference program's by a relative error of at most 0.0058.
Values may be sent and summed in bfloat16 or wider, within the bound.
A program may use at most 64 MiB of HBM per device.

```python
import jax
import jax.numpy as jnp
from jax import lax

C = 96
HID = 384
LAYERS = 2
CLON = 128
NLAT = 128
NLON = 8192


def draw_land_mask(key, part):
    key = jax.random.fold_in(key, 11)
    region_key, cell_key = jax.random.split(key)
    row_blocks = NLAT // 8
    col_blocks = NLON // CLON
    region_kind = jax.random.randint(region_key, (row_blocks, col_blocks), 0, 4)
    cell_draw = jax.random.randint(cell_key, (NLAT, NLON), 0, 4)
    region_full = jnp.repeat(jnp.repeat(region_kind, 8, axis=0), CLON, axis=1)
    ocean_cells = (region_full == 3) | (region_full > 0) & (cell_draw > 0)
    return ocean_cells.astype(jnp.int32)


def steps_of(rng, extent, cuts, least, high):
    gain, own = 1.0, jax.random.fold_in(rng, 6)
    for axis_at, parts in cuts:
        steps = jnp.exp(jax.random.uniform(jax.random.fold_in(own, axis_at), (parts,), jnp.float32, least / len(cuts), high / len(cuts)))
        gain = gain * jnp.repeat(steps, extent[axis_at] // parts).reshape([-1 if axis == axis_at else 1 for axis in range(len(extent))])
    return gain


def bell_draw(rng, extent, deviation, reach, pieces=(), held_as=jnp.bfloat16):
    values = jax.random.normal(rng, extent, jnp.float32) * deviation
    if len(pieces) > 0:
        values = steps_of(rng, extent, pieces, -0.22, 0.18) * values
    return jnp.clip(values, min=-reach, max=reach).astype(held_as)


def setup_inputs(seed: int = 0) -> dict:
    splits = jax.random.split(jax.random.key(seed), 11)
    field = bell_draw(splits[0], (C, NLAT, NLON), 1.0, 6.0, ((1, 8), (2, 64)))
    land_mask = draw_land_mask(jax.random.fold_in(splits[10], 71), 0)
    depth_kernel = bell_draw(splits[2], (LAYERS, C, 7, 7), 49 ** -0.5, 0.875, (), jnp.float32)
    depth_bias = bell_draw(splits[3], (LAYERS, C), 0.5, 3.0, (), jnp.float32)
    norm_gain = jnp.clip(1.0 + 0.18 * jax.random.normal(splits[4], (LAYERS, C), jnp.float32), 0.1, 1.9)
    norm_bias = bell_draw(splits[5], (LAYERS, C), 0.5, 3.0, (), jnp.float32)
    w_expand = bell_draw(splits[6], (LAYERS, HID, C), C ** -0.5, 0.625)
    b_expand = bell_draw(splits[7], (LAYERS, HID), 0.5, 3.0, (), jnp.float32)
    w_reduce = bell_draw(splits[8], (LAYERS, C, HID), HID ** -0.5, 0.3125)
    b_reduce = bell_draw(splits[9], (LAYERS, C), 0.5, 3.0, (), jnp.float32)
    return dict(field=field, land_mask=land_mask, depth_kernel=depth_kernel, depth_bias=depth_bias, norm_gain=norm_gain, norm_bias=norm_bias, w_expand=w_expand, b_expand=b_expand, w_reduce=w_reduce, b_reduce=b_reduce)


def extend(values):
    fold_rows = values[:, NLAT - 3:, :][:, ::-1, ::-1]
    bottom_rows = jnp.zeros((values.shape[0], 3, values.shape[2]), values.dtype)
    extended = jnp.concatenate([bottom_rows, values, fold_rows], axis=1)
    return jnp.concatenate([extended[:, :, -3:], extended, extended[:, :, :3]], axis=2)

def depthwise(band_rows, kernel, conv_bias):
    band_rows = band_rows.astype(jnp.float32)
    height = band_rows.shape[1] - 6
    width = band_rows.shape[2] - 6
    summed = jnp.zeros((band_rows.shape[0], height, width), jnp.float32) + conv_bias[:, None, None]
    for shift_row in range(7):
        for shift_col in range(7):
            summed = summed + kernel[:, shift_row, shift_col, None, None] * band_rows[:, shift_row:shift_row + height, shift_col:shift_col + width]
    return summed

def finish(mixed_cells, old_values, ocean_flags, norm_gain, norm_bias, w_expand, b_expand, w_reduce, b_reduce):
    channels, height, width = mixed_cells.shape
    flat_cells = mixed_cells.reshape(channels, height * width)
    average = lax.optimization_barrier(jnp.mean(flat_cells, axis=0))
    centered = flat_cells - average
    variance = lax.optimization_barrier(jnp.mean(centered * centered, axis=0))
    normed = (centered / jnp.sqrt(variance + 1e-06) * norm_gain[:, None] + norm_bias[:, None]).astype(jnp.bfloat16)
    hidden = jnp.dot(w_expand, normed, preferred_element_type=jnp.float32) + b_expand[:, None]
    hidden = jax.nn.gelu(hidden, approximate=False).astype(jnp.bfloat16)
    update = jnp.dot(w_reduce, hidden, preferred_element_type=jnp.float32) + b_reduce[:, None]
    flags = ocean_flags.reshape(height * width).astype(jnp.float32)
    result_band = flags[None, :] * (old_values.reshape(channels, height * width).astype(jnp.float32) + update)
    return result_band.astype(jnp.bfloat16).reshape(channels, height, width)

def convnext_layer(values, land_mask, kernel, conv_bias, norm_gain, norm_bias, w_expand, b_expand, w_reduce, b_reduce):
    extended = extend(values)

    def band_step(band):
        start = band * 8
        band_rows = lax.dynamic_slice_in_dim(extended, start, 14, 1)
        mixed_cells = depthwise(band_rows, kernel, conv_bias)
        old_values = lax.dynamic_slice_in_dim(values, start, 8, 1)
        ocean_flags = lax.dynamic_slice_in_dim(land_mask, start, 8, 0)
        return finish(mixed_cells, old_values, ocean_flags, norm_gain, norm_bias, w_expand, b_expand, w_reduce, b_reduce)
    bands = lax.map(band_step, jnp.arange(NLAT // 8, dtype=jnp.int32))
    return bands.transpose(1, 0, 2, 3).reshape(values.shape)

def reference(field, land_mask, depth_kernel, depth_bias, norm_gain, norm_bias, w_expand, b_expand, w_reduce, b_reduce):
    values = field
    for layer_index in range(LAYERS):
        values = convnext_layer(values, land_mask, depth_kernel[layer_index], depth_bias[layer_index], norm_gain[layer_index], norm_bias[layer_index], w_expand[layer_index], b_expand[layer_index], w_reduce[layer_index], b_reduce[layer_index])
    return values
```

```python
import functools

import jax
import jax.numpy as jnp
import numpy as np
from jax import lax
from jax.experimental import pallas as pl
from jax.experimental.pallas import tpu as pltpu
from jax.sharding import PartitionSpec as P

LAYERS = 2
C = 96
HID = 384
ROWS = 16
COLS = 128
GROUPS = C // 16
MESH = pl.DeviceIdType.MESH


def lane_ids(shape):
    return lax.broadcasted_iota(jnp.int32, shape, len(shape) - 1)


def build_weights(layer, vec, conv_w, colv):
    spread_shape = (COLS, 7 * COLS)
    tap = lax.broadcasted_iota(jnp.int32, spread_shape, 0)
    lane = lane_ids(spread_shape)
    rest = lane % COLS
    wanted = (rest // 16) * 7 + lane // COLS
    spread = jnp.where((tap == wanted) & (rest < 112), 1.0, 0.0).astype(jnp.bfloat16)
    taps = vec[layer].astype(jnp.bfloat16)
    flat = jnp.dot(taps, spread, preferred_element_type=jnp.float32)
    sub = lax.broadcasted_iota(jnp.int32, (C, COLS), 0)
    own = (lane_ids((C, COLS)) % 16) == (sub % 16)
    for d in range(7):
        band = jnp.where(own, flat[:, d * COLS : (d + 1) * COLS], 0.0)
        wide = jnp.concatenate([band, jnp.zeros_like(band)], axis=1)
        for r in range(10):
            moved = wide if r == 0 else pltpu.roll(wide, 16 * r, axis=1)
            moved = moved.astype(jnp.bfloat16)
            conv_w[layer, :, r * 16 : (r + 1) * 16, d * 256 : (d + 1) * 256] = moved.reshape(GROUPS, 16, 256)
    for k in range(4):
        colv[layer, k] = jnp.broadcast_to(vec[layer, :, 49 + k : 50 + k], (C, COLS))


def kernel(
    x_in, mask, vec, w_e, w_r, out,
    x_ext, pack, pack_l, pack_r, q_mid, q_up, q_down, mirror, q_mirror,
    conv_w, colv, shifted, mixed, send, recv,
):
    lat, lon = lax.axis_index("lat"), lax.axis_index("lon")
    nlat, nlon = lax.axis_size("lat"), lax.axis_size("lon")
    left = {"lat": lat, "lon": lax.rem(lon + nlon - 1, nlon)}
    right = {"lat": lat, "lon": lax.rem(lon + 1, nlon)}
    partner = {"lat": lat, "lon": nlon - 1 - lon}
    above = {"lat": jnp.minimum(lat + 1, nlat - 1), "lon": lon}
    below = {"lat": jnp.maximum(lat - 1, 0), "lon": lon}
    at_top = lat == nlat - 1
    not_top = lat < nlat - 1
    not_bottom = lat > 0
    barrier = pltpu.get_barrier_semaphore()

    def greet(device):
        pl.semaphore_signal(barrier, inc=1, device_id=device, device_id_type=MESH)

    greet(left)
    greet(right)
    pl.when(at_top)(lambda: greet(partner))
    pl.when(not_top)(lambda: greet(above))
    pl.when(not_bottom)(lambda: greet(below))

    lane = lane_ids((C, COLS))

    def fill_pack(layer):
        acc = pltpu.roll(x_ext[layer, 3], 3, axis=1)
        for r in range(1, ROWS):
            acc = jnp.where(lane // 8 == r, pltpu.roll(x_ext[layer, 3 + r], 8 * r + 3, axis=1), acc)
        pack[layer] = acc

    def fill_mirror(layer):
        rows = lax.broadcasted_iota(jnp.int32, (COLS, COLS), 0)
        flip = jnp.where(rows + lane_ids((COLS, COLS)) == COLS - 1, 1.0, 0.0).astype(jnp.bfloat16)
        for r in range(3):
            mirror[layer, r] = jnp.dot(
                x_ext[layer, 18 - r], flip, preferred_element_type=jnp.float32
            ).astype(jnp.bfloat16)

    def fill_q_mirror(layer):
        rows = lax.broadcasted_iota(jnp.int32, (COLS, COLS), 0)
        total = rows + lane_ids((COLS, COLS))
        flip = jnp.where((total == 125) | (total == 253), 1.0, 0.0).astype(jnp.bfloat16)
        q_mirror[layer] = jnp.dot(
            q_mid[layer], flip, preferred_element_type=jnp.float32
        ).astype(jnp.bfloat16)

    def remote(src, dst, slot, device):
        return pltpu.make_async_remote_copy(
            src_ref=src, dst_ref=dst, send_sem=send.at[slot], recv_sem=recv.at[slot],
            device_id=device, device_id_type=MESH,
        )

    def copy(layer, k):
        base = 8 * layer
        if k == 0:
            return remote(pack.at[layer], pack_r.at[layer], base, left)
        if k == 1:
            return remote(pack.at[layer], pack_l.at[layer], base + 1, right)
        if k == 2:
            return remote(x_ext.at[layer, pl.ds(3, 3)], x_ext.at[layer, pl.ds(19, 3)], base + 2, below)
        if k == 3:
            return remote(x_ext.at[layer, pl.ds(16, 3)], x_ext.at[layer, pl.ds(0, 3)], base + 3, above)
        if k == 4:
            return remote(q_mid.at[layer], q_up.at[layer], base + 4, below)
        if k == 5:
            return remote(q_mid.at[layer], q_down.at[layer], base + 5, above)
        if k == 6:
            return remote(mirror.at[layer], x_ext.at[layer, pl.ds(19, 3)], base + 6, partner)
        return remote(q_mirror.at[layer], q_up.at[layer], base + 7, partner)

    def send_first(layer):
        copy(layer, 0).start()
        copy(layer, 1).start()
        pl.when(not_bottom)(lambda: copy(layer, 2).start())
        pl.when(not_top)(lambda: copy(layer, 3).start())
        pl.when(at_top)(lambda: copy(layer, 6).start())

    def send_edges(layer):
        copy(layer, 0).wait_recv()
        copy(layer, 1).wait_recv()
        q_mid[layer] = jnp.where(lane % 8 >= 3, pack_r[layer], pack_l[layer])
        pl.when(not_bottom)(lambda: copy(layer, 4).start())
        pl.when(not_top)(lambda: copy(layer, 5).start())

        @pl.when(at_top)
        def _():
            fill_q_mirror(layer)
            copy(layer, 7).start()

    def wait_rows(layer):
        @pl.when(not_bottom)
        def _():
            copy(layer, 3).wait_recv()
            copy(layer, 5).wait_recv()

        @pl.when(lat == 0)
        def _():
            x_ext[layer, 0:3] = jnp.zeros((3, C, COLS), jnp.bfloat16)
            q_down[layer] = jnp.zeros((C, COLS), jnp.bfloat16)

        @pl.when(not_top)
        def _():
            copy(layer, 2).wait_recv()
            copy(layer, 4).wait_recv()

        @pl.when(at_top)
        def _():
            copy(layer, 6).wait_recv()
            copy(layer, 7).wait_recv()

    def wait_sends(layer):
        copy(layer, 0).wait_send()
        copy(layer, 1).wait_send()

        @pl.when(not_bottom)
        def _():
            copy(layer, 2).wait_send()
            copy(layer, 4).wait_send()

        @pl.when(not_top)
        def _():
            copy(layer, 3).wait_send()
            copy(layer, 5).wait_send()

        @pl.when(at_top)
        def _():
            copy(layer, 6).wait_send()
            copy(layer, 7).wait_send()

    def shift_row(layer, e, q, q_row):
        x = x_ext[layer, e]
        z = pltpu.roll(q, 2 * COLS - 3 - 8 * q_row, axis=1)
        for d in range(-3, 4):
            if d == 0:
                y = x
            else:
                outside = lane < d if d > 0 else lane >= COLS + d
                y = pltpu.roll(jnp.where(outside, z, x), (COLS - d) % COLS, axis=1)
            shifted[:, d + 3, e] = y.reshape(GROUPS, 16, COLS)

    def conv(layer, g, first, last, start):
        w = conv_w[layer, g, first * 16 : last * 16, :]
        x = shifted[g, :, start : start + 16].reshape(7 * 256, COLS)
        got = jnp.dot(w, x, preferred_element_type=jnp.float32)
        mixed[start + first : start + last, g] = got.reshape(last - first, 16, COLS)

    def two(v):
        return jnp.concatenate([v, v], axis=1)

    def mlp(layer, r0, r1):
        def both(pick):
            return jnp.concatenate([pick(r0), pick(r1)], axis=1)

        c = both(lambda r: mixed[r].reshape(C, COLS)) + two(colv[layer, 0])
        mean = jnp.sum(c, axis=0, keepdims=True) * (1.0 / C)
        c = c - mean
        var = jnp.sum(c * c, axis=0, keepdims=True) * (1.0 / C)
        n = c * lax.rsqrt(var + 1e-6) * two(colv[layer, 1]) + two(colv[layer, 2])
        ones = jnp.where(lax.broadcasted_iota(jnp.int32, (32, 2 * COLS), 0) < 2, 1.0, 0.0)
        n = jnp.concatenate([n, ones], axis=0).astype(jnp.bfloat16)
        h = jnp.dot(w_e[layer], n, preferred_element_type=jnp.float32)
        h = (0.5 * h * (1.0 + lax.erf(h * np.float32(np.sqrt(0.5))))).astype(jnp.bfloat16)
        u = jnp.dot(w_r[layer], h, preferred_element_type=jnp.float32) + two(colv[layer, 3])
        x = both(lambda r: x_ext[layer, 3 + r]).astype(jnp.float32)
        flags = both(lambda r: mask[pl.ds(r, 1), :]).astype(jnp.float32)
        y = (flags * (x + u)).astype(jnp.bfloat16)
        for k, r in enumerate((r0, r1)):
            part = y[:, k * COLS : (k + 1) * COLS]
            if layer == LAYERS - 1:
                out[r] = part
            else:
                x_ext[layer + 1, 3 + r] = part

    def loop(count, body):
        def step(i, carry):
            body(i)
            return carry

        lax.fori_loop(0, count, step, 0)

    def prepare(layer):
        fill_pack(layer)
        pl.when(at_top)(lambda: fill_mirror(layer))

    def spread_row(k):
        return k + 10 * ((k + 3) // 6)

    x_ext[0, 3:19] = x_in[...]
    prepare(0)
    pl.semaphore_wait(barrier, jnp.where(not_bottom, 4, 3))
    send_first(0)
    for layer in range(LAYERS):
        build_weights(layer, vec, conv_w, colv)
    for layer in range(LAYERS):
        if layer > 0:
            prepare(layer)
            send_first(layer)
        send_edges(layer)
        q = q_mid[layer]
        loop(ROWS, lambda r: shift_row(layer, r + 3, q, r))
        loop(GROUPS, lambda g: conv(layer, g, 0, 10, 3))
        loop(5, lambda k: mlp(layer, 2 * k + 3, 2 * k + 4))
        wait_rows(layer)
        for e in range(3):
            shift_row(layer, e, q_down[layer], 13 + e)
            shift_row(layer, 19 + e, q_up[layer], e)
        loop(GROUPS, lambda g: conv(layer, g, 0, 3, 0))
        loop(GROUPS, lambda g: conv(layer, g, 7, 10, 6))
        loop(3, lambda k: mlp(layer, spread_row(2 * k), spread_row(2 * k + 1)))
    for layer in range(LAYERS):
        wait_sends(layer)


def per_device(
    field, land_mask, depth_kernel, depth_bias, norm_gain, norm_bias, w_expand, b_expand, w_reduce, b_reduce
):
    x = jnp.transpose(field, (1, 0, 2))
    vec = jnp.concatenate(
        [depth_kernel.reshape(LAYERS, C, 49)]
        + [v[:, :, None] for v in (depth_bias, norm_gain, norm_bias, b_reduce)]
        + [jnp.zeros((LAYERS, C, COLS - 53), jnp.float32)],
        axis=2,
    )
    high = b_expand.astype(jnp.bfloat16)
    low = (b_expand - high.astype(jnp.float32)).astype(jnp.bfloat16)
    w_e = jnp.concatenate(
        [w_expand, high[:, :, None], low[:, :, None], jnp.zeros((LAYERS, HID, COLS - C - 2), jnp.bfloat16)], axis=2
    )
    tile = (LAYERS, C, COLS)
    bf = jnp.bfloat16
    vmem = pl.BlockSpec(memory_space=pltpu.VMEM)
    out = pl.pallas_call(
        kernel,
        out_shape=jax.ShapeDtypeStruct((ROWS, C, COLS), bf),
        in_specs=[vmem] * 5,
        out_specs=vmem,
        scratch_shapes=[
            pltpu.VMEM((LAYERS, ROWS + 6, C, COLS), bf),
            pltpu.VMEM(tile, bf),
            pltpu.VMEM(tile, bf),
            pltpu.VMEM(tile, bf),
            pltpu.VMEM(tile, bf),
            pltpu.VMEM(tile, bf),
            pltpu.VMEM(tile, bf),
            pltpu.VMEM((LAYERS, 3, C, COLS), bf),
            pltpu.VMEM(tile, bf),
            pltpu.VMEM((LAYERS, GROUPS, 160, 7 * 256), bf),
            pltpu.VMEM((LAYERS, 4, C, COLS), jnp.float32),
            pltpu.VMEM((GROUPS, 7, ROWS + 6, 16, COLS), bf),
            pltpu.VMEM((ROWS, GROUPS, 16, COLS), jnp.float32),
            pltpu.SemaphoreType.DMA((16,)),
            pltpu.SemaphoreType.DMA((16,)),
        ],
        compiler_params=pltpu.CompilerParams(
            collective_id=0, has_side_effects=True, vmem_limit_bytes=48 * 1024 * 1024
        ),
    )(x, land_mask, vec, w_e, w_reduce)
    return jnp.transpose(out, (1, 0, 2))


def solution(mesh):
    placed = (P(None, "lat", "lon"), P("lat", "lon"), P(), P(), P(), P(), P(), P(), P(), P())
    return jax.shard_map(
        per_device, mesh=mesh, in_specs=placed, out_specs=P(None, "lat", "lon"), check_vma=False
    )
```

```python
import jax
import jax.numpy as jnp
import numpy as np
from jax import lax
from jax.experimental import pallas as pl
from jax.experimental.pallas import tpu as pltpu
from jax.sharding import PartitionSpec as P

LAYERS = 2
C = 96
HID = 384
ROWS = 16
COLS = 128
GROUPS = C // 16
MESH = pl.DeviceIdType.MESH
BF = jnp.bfloat16
F32 = jnp.float32
SIDE = (0, 1, 2, 4, 5, 6)


def ids(shape, dim):
    return lax.broadcasted_iota(jnp.int32, shape, dim)


def kernel(
    field, mask_in, taps_in, dbias_in, gain_in, nbias_in, w_e_in, b_e_in, w_r_in, b_r_in, out,
    raw, mask, taps, dbias, gain, nbias, w_e_raw, b_e, w_r, b_r,
    cells, x_ext, pack, pack_l, pack_r, q_mid, q_up, q_down, mirror, q_mirror,
    table, w_e, conv_w, low_w, high_w, side_w, colv, shifted, mixed, edge, load, send, recv,
):
    lat, lon = lax.axis_index("lat"), lax.axis_index("lon")
    nlat, nlon = lax.axis_size("lat"), lax.axis_size("lon")
    left = {"lat": lat, "lon": lax.rem(lon + nlon - 1, nlon)}
    right = {"lat": lat, "lon": lax.rem(lon + 1, nlon)}
    partner = {"lat": lat, "lon": nlon - 1 - lon}
    above = {"lat": jnp.minimum(lat + 1, nlat - 1), "lon": lon}
    below = {"lat": jnp.maximum(lat - 1, 0), "lon": lon}
    at_top = lat == nlat - 1
    not_top = lat < nlat - 1
    not_bottom = lat > 0
    barrier = pltpu.get_barrier_semaphore()

    def greet(device):
        pl.semaphore_signal(barrier, inc=1, device_id=device, device_id_type=MESH)

    greet(left)
    greet(right)
    pl.when(at_top)(lambda: greet(partner))
    pl.when(not_top)(lambda: greet(above))
    pl.when(not_bottom)(lambda: greet(below))

    pairs = (
        (field, raw), (taps_in, taps), (dbias_in, dbias), (gain_in, gain), (nbias_in, nbias), (b_r_in, b_r),
        (w_e_in, w_e_raw), (b_e_in, b_e), (w_r_in, w_r), (mask_in, mask),
    )
    loads = [pltpu.make_async_copy(src, dst, load.at[k]) for k, (src, dst) in enumerate(pairs)]
    for one in loads:
        one.start()

    def remote(src, dst, slot, device):
        return pltpu.make_async_remote_copy(
            src_ref=src, dst_ref=dst, send_sem=send.at[slot], recv_sem=recv.at[slot],
            device_id=device, device_id_type=MESH,
        )

    def copy(layer, k):
        base = 8 * layer
        if k == 0:
            return remote(pack.at[layer], pack_r.at[layer], base, left)
        if k == 1:
            return remote(pack.at[layer], pack_l.at[layer], base + 1, right)
        if k == 2:
            return remote(x_ext.at[layer, pl.ds(3, 3)], x_ext.at[layer, pl.ds(19, 3)], base + 2, below)
        if k == 3:
            return remote(x_ext.at[layer, pl.ds(16, 3)], x_ext.at[layer, pl.ds(0, 3)], base + 3, above)
        if k == 4:
            return remote(q_mid.at[layer], q_up.at[layer], base + 4, below)
        if k == 5:
            return remote(q_mid.at[layer], q_down.at[layer], base + 5, above)
        if k == 6:
            return remote(mirror.at[layer], x_ext.at[layer, pl.ds(19, 3)], base + 6, partner)
        return remote(q_mirror.at[layer], q_up.at[layer], base + 7, partner)

    lane = ids((C, COLS), 1)

    def loop(count, body, unroll=1):
        def step(i, carry):
            body(i)
            return carry

        lax.fori_loop(0, count, step, 0, unroll=unroll)

    def flipped(value, total):
        away = (ids((COLS, COLS), 0) + ids((COLS, COLS), 1)) % COLS
        flip = jnp.where(away == total, 1.0, 0.0).astype(BF)
        return jnp.dot(value, flip, preferred_element_type=F32).astype(BF)

    def fill_pack(layer):
        acc = pltpu.roll(x_ext[layer, 3], 3, axis=1)
        for r in range(1, ROWS):
            acc = jnp.where(lane // 8 == r, pltpu.roll(x_ext[layer, 3 + r], 8 * r + 3, axis=1), acc)
        pack[layer] = acc

    def fill_mirror(layer):
        for r in range(3):
            mirror[layer, r] = flipped(x_ext[layer, 18 - r], COLS - 1)

    def send_strips(layer):
        pl.when(not_bottom)(lambda: copy(layer, 2).start())
        pl.when(not_top)(lambda: copy(layer, 3).start())

        @pl.when(at_top)
        def _():
            fill_mirror(layer)
            copy(layer, 6).start()

    def send_pack(layer):
        fill_pack(layer)
        copy(layer, 0).start()
        copy(layer, 1).start()

    def send_edges(layer):
        copy(layer, 0).wait_recv()
        copy(layer, 1).wait_recv()
        q_mid[layer] = jnp.where(lane % 8 >= 3, pack_r[layer], pack_l[layer])
        pl.when(not_bottom)(lambda: copy(layer, 4).start())
        pl.when(not_top)(lambda: copy(layer, 5).start())

        @pl.when(at_top)
        def _():
            q_mirror[layer] = flipped(q_mid[layer], 125)
            copy(layer, 7).start()

    def wait_rows(layer):
        @pl.when(not_bottom)
        def _():
            copy(layer, 3).wait_recv()
            copy(layer, 5).wait_recv()

        @pl.when(lat == 0)
        def _():
            x_ext[layer, 0:3] = jnp.zeros((3, C, COLS), BF)
            q_down[layer] = jnp.zeros((C, COLS), BF)

        @pl.when(not_top)
        def _():
            copy(layer, 2).wait_recv()
            copy(layer, 4).wait_recv()

        @pl.when(at_top)
        def _():
            copy(layer, 6).wait_recv()
            copy(layer, 7).wait_recv()

    def wait_sends(layer):
        copy(layer, 0).wait_send()
        copy(layer, 1).wait_send()

        @pl.when(not_bottom)
        def _():
            copy(layer, 2).wait_send()
            copy(layer, 4).wait_send()

        @pl.when(not_top)
        def _():
            copy(layer, 3).wait_send()
            copy(layer, 5).wait_send()

        @pl.when(at_top)
        def _():
            copy(layer, 6).wait_send()
            copy(layer, 7).wait_send()

    def build_weights(layer):
        table[...] = jnp.zeros((COLS, COLS), F32)
        table[0:49, 0:C] = taps[:, layer, :]
        for k, v in enumerate((dbias, gain, nbias, b_r)):
            table[49 + k : 50 + k, 0:C] = v[layer : layer + 1, :]
        vec = jnp.transpose(table[...])[0:C]
        for k in range(4):
            colv[layer, k] = jnp.broadcast_to(vec[:, 49 + k : 50 + k], (C, COLS))
        vec = vec.astype(BF)
        bias = b_e[layer : layer + 1, :]
        high = bias.astype(BF).astype(F32)
        wide = jnp.concatenate(
            [w_e_raw[layer].astype(F32), high, bias - high, jnp.zeros((COLS - C - 2, HID), F32)], axis=0
        )
        w_e[layer] = (0.5 * jnp.transpose(wide)).astype(BF)
        shape = (COLS, 7 * COLS)
        at = ids(shape, 1)
        rest = at % COLS
        spread = jnp.where((ids(shape, 0) == (rest // 16) * 7 + at // COLS) & (rest < 112), 1.0, 0.0).astype(BF)
        flat = jnp.dot(vec, spread, preferred_element_type=F32)
        own = (lane % 16) == (ids((C, COLS), 0) % 16)
        for d in range(7):
            band = jnp.where(own, flat[:, d * COLS : (d + 1) * COLS], 0.0)
            none = jnp.zeros_like(band)
            for r in range(ROWS):
                by = 16 * (r - 3)
                turned = band if by % COLS == 0 else pltpu.roll(band, by % COLS, axis=1)
                if by < 0:
                    low, high = jnp.where(lane < COLS + by, turned, 0.0), none
                elif by < COLS:
                    low, high = jnp.where(lane >= by, turned, 0.0), jnp.where(lane < by, turned, 0.0)
                else:
                    low, high = none, jnp.where(lane >= by - COLS, turned, 0.0)
                at_rows = slice(r * 16, (r + 1) * 16)
                conv_w[layer, :, at_rows, d * 256 : d * 256 + 128] = low.astype(BF).reshape(GROUPS, 16, COLS)
                conv_w[layer, :, at_rows, d * 256 + 128 : d * 256 + 256] = high.astype(BF).reshape(GROUPS, 16, COLS)
            for r in range(3):
                at_rows = slice(r * 16, (r + 1) * 16)
                turned = band if r == 0 else pltpu.roll(band, 16 * r, axis=1)
                part = jnp.where((lane >= 16 * r) & (lane < 48), turned, 0.0)
                low_w[layer, :, at_rows, d * 128 : d * 128 + 128] = part.astype(BF).reshape(GROUPS, 16, COLS)
                turned = band if r == 1 else pltpu.roll(band, (16 * r - 16) % COLS, axis=1)
                part = jnp.where((lane >= 80) & (lane < (112 if r == 0 else COLS)), turned, 0.0)
                high_w[layer, :, at_rows, d * 128 : d * 128 + 128] = part.astype(BF).reshape(GROUPS, 16, COLS)
        for k, d in enumerate(SIDE):
            shape = (COLS, 7 * COLS)
            at = ids(shape, 1)
            to = at % 8
            start = to + d - 3
            if d > 3:
                reach = (to < 3) & (start >= 3) & (start < 6)
            else:
                reach = (to >= 3) & (to < 6) & (start >= 0) & (start < 3)
            pick = jnp.where((ids(shape, 0) == (at // COLS) * 7 + d) & reach, 1.0, 0.0).astype(BF)
            got = jnp.dot(vec, pick, preferred_element_type=F32)
            for a in range(7):
                side_w[layer, k * 7 + a] = got[:, a * COLS : (a + 1) * COLS]

    def shift_own(layer, r):
        x = x_ext[layer, 3 + r]
        for d in range(-3, 4):
            y = x if d == 0 else pltpu.roll(x, (COLS - d) % COLS, axis=1)
            shifted[:, d + 3, 3 + r] = y.reshape(GROUPS, 16, COLS)

    def shift_halo(layer, e, q, q_row):
        x = x_ext[layer, e]
        z = pltpu.roll(q, 2 * COLS - 3 - 8 * q_row, axis=1)
        for d in range(-3, 4):
            if d == 0:
                y = x
            else:
                outside = lane < d if d > 0 else lane >= COLS + d
                y = pltpu.roll(jnp.where(outside, z, x), (COLS - d) % COLS, axis=1)
            shifted[:, d + 3, e] = y.reshape(GROUPS, 16, COLS)

    def conv_own(layer, g):
        x = shifted[g, :, 3:19].reshape(7 * 256, COLS)
        got = jnp.dot(conv_w[layer, g], x, preferred_element_type=F32)
        mixed[:, g] = got.reshape(ROWS, 16, COLS)

    def conv_halo(layer, g):
        x = shifted[g, :, 0:8].reshape(7 * 128, COLS)
        got = jnp.dot(low_w[layer, g], x, preferred_element_type=F32)
        mixed[0:3, g] += got.reshape(3, 16, COLS)
        x = shifted[g, :, 14:22].reshape(7 * 128, COLS)
        got = jnp.dot(high_w[layer, g], x, preferred_element_type=F32)
        mixed[13:16, g] += got.reshape(3, 16, COLS)

    def fill_edge(layer):
        delta = q_mid[layer].astype(F32) - pack[layer].astype(F32)
        total = jnp.zeros((C, COLS), F32)
        for a in range(7):
            by = 8 * (a - 3)
            if by > 0:
                rows = jnp.where(lane < by, 0.0, delta)
            elif by < 0:
                rows = jnp.where(lane >= COLS + by, 0.0, delta)
            else:
                rows = delta
            for k, d in enumerate(SIDE):
                total += side_w[layer, k * 7 + a] * pltpu.roll(rows, (3 * COLS - by - (d - 3)) % COLS, axis=1)
        edge[...] = total

    def two(v):
        return jnp.concatenate([v, v], axis=1)

    def mlp(layer, r0, r1):
        def both(pick):
            return jnp.concatenate([pick(r0), pick(r1)], axis=1)

        def rows(r):
            beside = pltpu.roll(edge[...], 2 * COLS - 3 - 8 * r, axis=1)
            return mixed[r].reshape(C, COLS) + jnp.where((lane < 3) | (lane >= COLS - 3), beside, 0.0)

        c = both(rows) + two(colv[layer, 0])
        mean = jnp.sum(c, axis=0, keepdims=True) * (1.0 / C)
        c = c - mean
        var = jnp.sum(c * c, axis=0, keepdims=True) * (1.0 / C)
        n = c * lax.rsqrt(var + 1e-6) * two(colv[layer, 1]) + two(colv[layer, 2])
        ones = jnp.where(ids((32, 2 * COLS), 0) < 2, 1.0, 0.0)
        n = jnp.concatenate([n, ones], axis=0).astype(BF)
        half = jnp.dot(w_e[layer], n, preferred_element_type=F32)
        h = (half + half * lax.erf(half * np.float32(np.sqrt(2.0)))).astype(BF)
        u = jnp.dot(w_r[layer], h, preferred_element_type=F32) + two(colv[layer, 3])
        x = both(lambda r: x_ext[layer, 3 + r]).astype(F32)
        flags = both(lambda r: mask[pl.ds(r, 1), :]).astype(F32)
        y = flags * (x + u)
        for k, r in enumerate((r0, r1)):
            part = y[:, k * COLS : (k + 1) * COLS]
            if layer == LAYERS - 1:
                cells[pl.ds(r, C, stride=ROWS), :] = part
            else:
                x_ext[layer + 1, 3 + r] = part.astype(BF)

    def spread_row(k):
        return k + 10 * ((k + 3) // 6)

    loads[0].wait()
    cells[...] = raw[...].astype(F32).reshape(C * ROWS, COLS)
    for r in range(ROWS):
        x_ext[0, 3 + r] = cells[pl.ds(r, C, stride=ROWS), :].astype(BF)
    fill_pack(0)
    pl.semaphore_wait(barrier, jnp.where(not_bottom, 4, 3))
    copy(0, 0).start()
    copy(0, 1).start()
    send_strips(0)
    for one in loads[1:]:
        one.wait()
    for layer in range(LAYERS):
        build_weights(layer)
    for layer in range(LAYERS):
        if layer > 0:
            send_strips(layer)
            send_pack(layer)
        loop(ROWS, lambda r: shift_own(layer, r), 4)
        send_edges(layer)
        loop(GROUPS, lambda g: conv_own(layer, g), 6)
        fill_edge(layer)
        loop(5, lambda k: mlp(layer, 2 * k + 3, 2 * k + 4), 5)
        wait_rows(layer)
        for e in range(3):
            shift_halo(layer, e, q_down[layer], 13 + e)
            shift_halo(layer, 19 + e, q_up[layer], e)
        loop(GROUPS, lambda g: conv_halo(layer, g), 6)
        loop(3, lambda k: mlp(layer, spread_row(2 * k), spread_row(2 * k + 1)), 3)
    out[...] = cells[...].reshape(C, ROWS, COLS).astype(BF)
    for layer in range(LAYERS):
        wait_sends(layer)


def per_device(
    field, land_mask, depth_kernel, depth_bias, norm_gain, norm_bias, w_expand, b_expand, w_reduce, b_reduce
):
    taps = jnp.transpose(depth_kernel, (2, 3, 0, 1)).reshape(49, LAYERS, C)
    args = (
        field, land_mask, taps, depth_bias, norm_gain, norm_bias, jnp.transpose(w_expand, (0, 2, 1)), b_expand,
        w_reduce, b_reduce,
    )
    tile = (LAYERS, C, COLS)
    held = [pltpu.VMEM(a.shape, a.dtype) for a in args]
    scratch = held + [
        pltpu.VMEM((C * ROWS, COLS), F32),
        pltpu.VMEM((LAYERS, ROWS + 6, C, COLS), BF),
    ]
    scratch += [pltpu.VMEM(tile, BF)] * 6
    scratch += [
        pltpu.VMEM((LAYERS, 3, C, COLS), BF),
        pltpu.VMEM(tile, BF),
        pltpu.VMEM((COLS, COLS), F32),
        pltpu.VMEM((LAYERS, HID, COLS), BF),
        pltpu.VMEM((LAYERS, GROUPS, 256, 7 * 256), BF),
        pltpu.VMEM((LAYERS, GROUPS, 48, 7 * 128), BF),
        pltpu.VMEM((LAYERS, GROUPS, 48, 7 * 128), BF),
        pltpu.VMEM((LAYERS, 42, C, COLS), F32),
        pltpu.VMEM((LAYERS, 4, C, COLS), F32),
        pltpu.VMEM((GROUPS, 7, ROWS + 6, 16, COLS), BF),
        pltpu.VMEM((ROWS, GROUPS, 16, COLS), F32),
        pltpu.VMEM((C, COLS), F32),
        pltpu.SemaphoreType.DMA((len(args),)),
        pltpu.SemaphoreType.DMA((16,)),
        pltpu.SemaphoreType.DMA((16,)),
    ]
    return pl.pallas_call(
        kernel,
        out_shape=jax.ShapeDtypeStruct((C, ROWS, COLS), BF),
        in_specs=[pl.BlockSpec(memory_space=pl.ANY)] * len(args),
        out_specs=pl.BlockSpec(memory_space=pltpu.VMEM),
        scratch_shapes=scratch,
        compiler_params=pltpu.CompilerParams(
            collective_id=0, has_side_effects=True, vmem_limit_bytes=56 * 1024 * 1024
        ),
    )(*args)


def solution(mesh):
    placed = (P(None, "lat", "lon"), P("lat", "lon"), P(), P(), P(), P(), P(), P(), P(), P())
    return jax.shard_map(
        per_device, mesh=mesh, in_specs=placed, out_specs=P(None, "lat", "lon"), check_vma=False
    )
```

```python
import jax
import jax.numpy as jnp
import numpy as np
from jax import lax
from jax.experimental import pallas as pl
from jax.experimental.pallas import tpu as pltpu
from jax.sharding import PartitionSpec as P

LAYERS = 2
C = 96
HID = 384
ROWS = 16
COLS = 128
GROUPS = C // 16
MESH = pl.DeviceIdType.MESH
BF = jnp.bfloat16
F32 = jnp.float32
SIDE = (0, 1, 2, 4, 5, 6)


def ids(shape, dim):
    return lax.broadcasted_iota(jnp.int32, shape, dim)


def kernel(
    field, mask_in, taps_in, dbias_in, gain_in, nbias_in, w_e_in, b_e_in, w_r_in, b_r_in, out,
    raw, mask, taps, dbias, gain, nbias, w_e_raw, b_e, w_r, b_r,
    cells, x_ext, pack, pack_l, pack_r, q_mid, q_halo, mirror, corner, corner_m, halo_t,
    table, w_e, conv_w, low_w, high_w, side_w, colv, shifted, mixed, edge, load, send, recv,
):
    lat, lon = lax.axis_index("lat"), lax.axis_index("lon")
    nlat, nlon = lax.axis_size("lat"), lax.axis_size("lon")
    lon_l, lon_r = lax.rem(lon + nlon - 1, nlon), lax.rem(lon + 1, nlon)
    lat_u, lat_d = jnp.minimum(lat + 1, nlat - 1), jnp.maximum(lat - 1, 0)
    fold_r, fold_l = lax.rem(2 * nlon - 2 - lon, nlon), lax.rem(nlon - lon, nlon)
    at_top = lat == nlat - 1
    not_top = lat < nlat - 1
    not_bottom = lat > 0
    fold_r_away = at_top & (fold_r != lon)
    fold_l_away = at_top & (fold_l != lon)
    left = {"lat": lat, "lon": lon_l}
    right = {"lat": lat, "lon": lon_r}
    peers = (
        (left, None), (right, None),
        ({"lat": lat_d, "lon": lon}, not_bottom),
        ({"lat": lat_d, "lon": lon_l}, not_bottom),
        ({"lat": lat_d, "lon": lon_r}, not_bottom),
        ({"lat": lat_u, "lon": lon}, not_top),
        ({"lat": lat_u, "lon": lon_l}, not_top),
        ({"lat": lat_u, "lon": lon_r}, not_top),
        ({"lat": lat, "lon": nlon - 1 - lon}, at_top),
        ({"lat": lat, "lon": fold_r}, fold_r_away),
        ({"lat": lat, "lon": fold_l}, fold_l_away),
    )
    barrier = pltpu.get_barrier_semaphore()

    def when(condition, body):
        if condition is None:
            body()
        else:
            pl.when(condition)(body)

    for device, condition in peers:
        when(
            condition,
            lambda: pl.semaphore_signal(barrier, inc=1, device_id=device, device_id_type=MESH),
        )
    n_peers = sum(1 if c is None else c.astype(jnp.int32) for _, c in peers)

    pairs = (
        (field, raw), (taps_in, taps), (dbias_in, dbias), (gain_in, gain), (nbias_in, nbias), (b_r_in, b_r),
        (w_e_in, w_e_raw), (b_e_in, b_e), (w_r_in, w_r), (mask_in, mask),
    )
    loads = [pltpu.make_async_copy(src, dst, load.at[k]) for k, (src, dst) in enumerate(pairs)]
    for one in loads:
        one.start()

    def remote(src, dst, slot, device):
        return pltpu.make_async_remote_copy(
            src_ref=src, dst_ref=dst, send_sem=send.at[slot], recv_sem=recv.at[slot],
            device_id=device, device_id_type=MESH,
        )

    def copy(layer, k):
        src, dst = (
            (pack.at[layer], pack_r.at[layer]),
            (pack.at[layer], pack_l.at[layer]),
            (x_ext.at[layer, pl.ds(3, 3)], x_ext.at[layer, pl.ds(19, 3)]),
            (corner.at[layer, pl.ds(0, 32)], halo_t.at[layer, 1, pl.ds(0, 32)]),
            (corner.at[layer, pl.ds(0, 32)], halo_t.at[layer, 0, pl.ds(0, 32)]),
            (x_ext.at[layer, pl.ds(16, 3)], x_ext.at[layer, pl.ds(0, 3)]),
            (corner.at[layer, pl.ds(96, 32)], halo_t.at[layer, 1, pl.ds(96, 32)]),
            (corner.at[layer, pl.ds(96, 32)], halo_t.at[layer, 0, pl.ds(96, 32)]),
            (mirror.at[layer], x_ext.at[layer, pl.ds(19, 3)]),
            (corner_m.at[layer], halo_t.at[layer, 1, pl.ds(0, 32)]),
            (corner_m.at[layer], halo_t.at[layer, 0, pl.ds(0, 32)]),
        )[k]
        return remote(src, dst, 11 * layer + k, peers[k][0])

    def start(layer, *numbers):
        for k in numbers:
            when(peers[k][1], lambda: copy(layer, k).start())

    def wait_recv(layer, *numbers):
        for k in numbers:
            condition = {2: not_top, 3: not_top, 4: not_top, 5: not_bottom, 6: not_bottom, 7: not_bottom}.get(k, peers[k][1])
            when(condition, lambda: copy(layer, k).wait_recv())

    def wait_sends(layer):
        for k in range(11):
            when(peers[k][1], lambda: copy(layer, k).wait_send())

    lane = ids((C, COLS), 1)

    def loop(count, body, unroll=1):
        def step(i, carry):
            body(i)
            return carry

        lax.fori_loop(0, count, step, 0, unroll=unroll)

    def add_pack(layer, rows, fresh=False):
        acc = None if fresh else pack[layer]
        for r in rows:
            turned = pltpu.roll(x_ext[layer, 3 + r], 8 * r + 3, axis=1)
            acc = turned if acc is None else jnp.where(lane // 8 == r, turned, acc)
        pack[layer] = acc

    def pick_lanes(rows, total):
        at, lanes = ids((rows, COLS), 0), ids((rows, COLS), 1)
        wanted = at if total is None else (total + COLS - at) % COLS
        return jnp.where(lanes == wanted, 1.0, 0.0).astype(BF)

    def fill_corner(layer):
        wide = jnp.concatenate([pack[layer], jnp.zeros((COLS - C, COLS), BF)], axis=0)

        def pick(rows, total):
            return lax.dot_general(
                pick_lanes(rows, total), wide, (((1,), (1,)), ((), ())), preferred_element_type=F32
            ).astype(BF)

        corner[layer] = pick(COLS, None)

        @pl.when(at_top)
        def _():
            corner_m[layer] = pick(32, 125)

        @pl.when(at_top & (fold_r == lon))
        def _():
            halo_t[layer, 1, 0:32] = corner_m[layer]

        @pl.when(at_top & (fold_l == lon))
        def _():
            halo_t[layer, 0, 0:32] = corner_m[layer]

    def send_low(layer):
        start(layer, 2)

    def send_high(layer):
        start(layer, 5)

        @pl.when(at_top)
        def _():
            flip = jnp.where(ids((COLS, COLS), 0) + ids((COLS, COLS), 1) == COLS - 1, 1.0, 0.0).astype(BF)
            rows = x_ext[layer, 16:19].reshape(3 * C, COLS)
            got = jnp.dot(rows, flip, preferred_element_type=F32).astype(BF)
            for r in range(3):
                mirror[layer, r] = got[(2 - r) * C : (3 - r) * C]
            copy(layer, 8).start()

    def send_pack(layer):
        start(layer, 0, 1)
        fill_corner(layer)
        start(layer, 3, 4, 6, 7, 9, 10)

    def take_pack(layer):
        wait_recv(layer, 0, 1)
        q_mid[layer] = jnp.where(lane % 8 >= 3, pack_r[layer], pack_l[layer])

    def take_corners(layer):
        wait_recv(layer, 3, 4, 6, 7, 9, 10)
        at = ids((COLS, COLS), 0)
        low = jnp.where(not_bottom, 96, COLS)
        both = jnp.where(at % 8 >= 3, halo_t[layer, 1].astype(F32), halo_t[layer, 0].astype(F32))
        both = jnp.where((at < 32) | (at >= low), both, 0.0).astype(BF)
        pick = jnp.where(ids((C, COLS), 0) == lane, 1.0, 0.0).astype(BF)
        q_halo[layer] = lax.dot_general(pick, both, (((1,), (1,)), ((), ())), preferred_element_type=F32).astype(BF)

    def take_low(layer):
        wait_recv(layer, 5)

        @pl.when(lat == 0)
        def _():
            x_ext[layer, 0:3] = jnp.zeros((3, C, COLS), BF)

    def take_high(layer):
        wait_recv(layer, 2, 8)

    def build_weights(layer):
        table[...] = jnp.zeros((COLS, COLS), F32)
        table[0:49, 0:C] = taps[:, layer, :]
        for k, v in enumerate((dbias, gain, nbias, b_r)):
            table[49 + k : 50 + k, 0:C] = v[layer : layer + 1, :]
        vec = jnp.transpose(table[...])[0:C]
        for k in range(4):
            colv[layer, k] = jnp.broadcast_to(vec[:, 49 + k : 50 + k], (C, COLS))
        vec = vec.astype(BF)
        bias = b_e[layer : layer + 1, :]
        high = bias.astype(BF).astype(F32)
        wide = jnp.concatenate(
            [w_e_raw[layer].astype(F32), high, bias - high, jnp.zeros((COLS - C - 2, HID), F32)], axis=0
        )
        w_e[layer] = (0.5 * jnp.transpose(wide)).astype(BF)
        shape = (COLS, 7 * COLS)
        at = ids(shape, 1)
        rest = at % COLS
        spread = jnp.where((ids(shape, 0) == (rest // 16) * 7 + at // COLS) & (rest < 112), 1.0, 0.0).astype(BF)
        flat = jnp.dot(vec, spread, preferred_element_type=F32)
        own = (lane % 16) == (ids((C, COLS), 0) % 16)
        for d in range(7):
            band = jnp.where(own, flat[:, d * COLS : (d + 1) * COLS], 0.0).astype(BF)
            none, zero = jnp.zeros_like(band), jnp.zeros((), BF)
            for r in range(ROWS):
                by = 16 * (r - 3)
                turned = band if by % COLS == 0 else pltpu.roll(band, by % COLS, axis=1)
                if by < 0:
                    low, high = jnp.where(lane < COLS + by, turned, zero), none
                elif by < COLS:
                    low, high = jnp.where(lane >= by, turned, zero), jnp.where(lane < by, turned, zero)
                else:
                    low, high = none, jnp.where(lane >= by - COLS, turned, zero)
                at_rows = slice(r * 16, (r + 1) * 16)
                conv_w[layer, :, at_rows, d * 256 : d * 256 + 128] = low.reshape(GROUPS, 16, COLS)
                conv_w[layer, :, at_rows, d * 256 + 128 : d * 256 + 256] = high.reshape(GROUPS, 16, COLS)
            for r in range(3):
                at_rows = slice(r * 16, (r + 1) * 16)
                turned = band if r == 0 else pltpu.roll(band, 16 * r, axis=1)
                part = jnp.where((lane >= 16 * r) & (lane < 48), turned, zero)
                low_w[layer, :, at_rows, d * 128 : d * 128 + 128] = part.reshape(GROUPS, 16, COLS)
                turned = band if r == 1 else pltpu.roll(band, (16 * r - 16) % COLS, axis=1)
                part = jnp.where((lane >= 80) & (lane < (112 if r == 0 else COLS)), turned, zero)
                high_w[layer, :, at_rows, d * 128 : d * 128 + 128] = part.reshape(GROUPS, 16, COLS)
        for k, d in enumerate(SIDE):
            shape = (COLS, 7 * COLS)
            at = ids(shape, 1)
            to = at % 8
            start = to + d - 3
            if d > 3:
                reach = (to < 3) & (start >= 3) & (start < 6)
            else:
                reach = (to >= 3) & (to < 6) & (start >= 0) & (start < 3)
            pick = jnp.where((ids(shape, 0) == (at // COLS) * 7 + d) & reach, 1.0, 0.0).astype(BF)
            got = jnp.dot(vec, pick, preferred_element_type=F32)
            for a in range(7):
                side_w[layer, k * 7 + a] = got[:, a * COLS : (a + 1) * COLS]

    def shift_own(layer, r):
        x = x_ext[layer, 3 + r]
        for d in range(-3, 4):
            y = x if d == 0 else pltpu.roll(x, (COLS - d) % COLS, axis=1)
            shifted[:, d + 3, 3 + r] = y.reshape(GROUPS, 16, COLS)

    def shift_halo(layer, e, q, q_row):
        x = x_ext[layer, e]
        z = pltpu.roll(q, 2 * COLS - 3 - 8 * q_row, axis=1)
        for d in range(-3, 4):
            if d == 0:
                y = x
            else:
                outside = lane < d if d > 0 else lane >= COLS + d
                y = pltpu.roll(jnp.where(outside, z, x), (COLS - d) % COLS, axis=1)
            shifted[:, d + 3, e] = y.reshape(GROUPS, 16, COLS)

    def conv_own(layer, g):
        x = shifted[g, :, 3:19].reshape(7 * 256, COLS)
        got = jnp.dot(conv_w[layer, g], x, preferred_element_type=F32)
        mixed[:, g] = got.reshape(ROWS, 16, COLS)

    def conv_low(layer, g):
        x = shifted[g, :, 0:8].reshape(7 * 128, COLS)
        got = jnp.dot(low_w[layer, g], x, preferred_element_type=F32)
        mixed[0:3, g] += got.reshape(3, 16, COLS)

    def conv_high(layer, g):
        x = shifted[g, :, 14:22].reshape(7 * 128, COLS)
        got = jnp.dot(high_w[layer, g], x, preferred_element_type=F32)
        mixed[13:16, g] += got.reshape(3, 16, COLS)

    def fill_edge(layer):
        delta = q_mid[layer].astype(F32) - pack[layer].astype(F32)
        total = jnp.zeros((C, COLS), F32)
        for a in range(7):
            by = 8 * (a - 3)
            if by > 0:
                rows = jnp.where(lane < by, 0.0, delta)
            elif by < 0:
                rows = jnp.where(lane >= COLS + by, 0.0, delta)
            else:
                rows = delta
            for k, d in enumerate(SIDE):
                total += side_w[layer, k * 7 + a] * pltpu.roll(rows, (3 * COLS - by - (d - 3)) % COLS, axis=1)
        edge[...] = total

    def mlp(layer, at_rows):
        count = len(at_rows)

        def each(pick):
            return jnp.concatenate([pick(r) for r in at_rows], axis=1)

        def same(v):
            return jnp.concatenate([v] * count, axis=1)

        def mixed_row(r):
            beside = pltpu.roll(edge[...], (2 * COLS - 3 - 8 * r) % COLS, axis=1)
            return mixed[r].reshape(C, COLS) + jnp.where((lane < 3) | (lane >= COLS - 3), beside, 0.0)

        c = each(mixed_row) + same(colv[layer, 0])
        mean = jnp.sum(c, axis=0, keepdims=True) * (1.0 / C)
        c = c - mean
        var = jnp.sum(c * c, axis=0, keepdims=True) * (1.0 / C)
        n = c * lax.rsqrt(var + 1e-6) * same(colv[layer, 1]) + same(colv[layer, 2])
        ones = jnp.where(ids((32, count * COLS), 0) < 2, 1.0, 0.0)
        n = jnp.concatenate([n, ones], axis=0).astype(BF)
        half = jnp.dot(w_e[layer], n, preferred_element_type=F32)
        h = (half + half * lax.erf(half * np.float32(np.sqrt(2.0)))).astype(BF)
        u = jnp.dot(w_r[layer], h, preferred_element_type=F32) + same(colv[layer, 3])
        x = each(lambda r: x_ext[layer, 3 + r]).astype(F32)
        flags = each(lambda r: mask[r : r + 1, :]).astype(F32)
        y = flags * (x + u)
        for k, r in enumerate(at_rows):
            part = y[:, k * COLS : (k + 1) * COLS]
            if layer == LAYERS - 1:
                cells[pl.ds(r, C, stride=ROWS), :] = part
            else:
                x_ext[layer + 1, 3 + r] = part.astype(BF)

    loads[0].wait()
    cells[...] = raw[...].astype(F32).reshape(C * ROWS, COLS)
    for r in range(ROWS):
        x_ext[0, 3 + r] = cells[pl.ds(r, C, stride=ROWS), :].astype(BF)
    add_pack(0, range(ROWS), fresh=True)
    pl.semaphore_wait(barrier, n_peers)
    send_low(0)
    send_high(0)
    send_pack(0)
    for one in loads[1:]:
        one.wait()
    for layer in range(LAYERS):
        build_weights(layer)
    for layer in range(LAYERS):
        onward = layer + 1 < LAYERS
        loop(ROWS, lambda r: shift_own(layer, r), 4)
        loop(GROUPS, lambda g: conv_own(layer, g), GROUPS)
        take_pack(layer)
        fill_edge(layer)
        for r in range(3, 13, 2):
            mlp(layer, (r, r + 1))
        if onward:
            add_pack(layer + 1, range(3, 13), fresh=True)
        take_corners(layer)
        take_low(layer)
        for e in range(3):
            shift_halo(layer, e, q_halo[layer], 13 + e)
        loop(GROUPS, lambda g: conv_low(layer, g), GROUPS)
        mlp(layer, (0, 1, 2))
        if onward:
            send_low(layer + 1)
        take_high(layer)
        for e in range(3):
            shift_halo(layer, 19 + e, q_halo[layer], e)
        loop(GROUPS, lambda g: conv_high(layer, g), GROUPS)
        mlp(layer, (13, 14, 15))
        if onward:
            send_high(layer + 1)
            add_pack(layer + 1, (0, 1, 2, 13, 14, 15))
            send_pack(layer + 1)
    out[...] = cells[...].reshape(C, ROWS, COLS).astype(BF)
    for layer in range(LAYERS):
        wait_sends(layer)


def per_device(
    field, land_mask, depth_kernel, depth_bias, norm_gain, norm_bias, w_expand, b_expand, w_reduce, b_reduce
):
    taps = jnp.transpose(depth_kernel, (2, 3, 0, 1)).reshape(49, LAYERS, C)
    args = (
        field, land_mask, taps, depth_bias, norm_gain, norm_bias, jnp.transpose(w_expand, (0, 2, 1)), b_expand,
        w_reduce, b_reduce,
    )
    tile = (LAYERS, C, COLS)
    held = [pltpu.VMEM(a.shape, a.dtype) for a in args]
    scratch = held + [
        pltpu.VMEM((C * ROWS, COLS), F32),
        pltpu.VMEM((LAYERS, ROWS + 6, C, COLS), BF),
    ]
    scratch += [pltpu.VMEM(tile, BF)] * 5
    scratch += [
        pltpu.VMEM((LAYERS, 3, C, COLS), BF),
        pltpu.VMEM((LAYERS, COLS, COLS), BF),
        pltpu.VMEM((LAYERS, 32, COLS), BF),
        pltpu.VMEM((LAYERS, 2, COLS, COLS), BF),
        pltpu.VMEM((COLS, COLS), F32),
        pltpu.VMEM((LAYERS, HID, COLS), BF),
        pltpu.VMEM((LAYERS, GROUPS, 256, 7 * 256), BF),
        pltpu.VMEM((LAYERS, GROUPS, 48, 7 * 128), BF),
        pltpu.VMEM((LAYERS, GROUPS, 48, 7 * 128), BF),
        pltpu.VMEM((LAYERS, 42, C, COLS), F32),
        pltpu.VMEM((LAYERS, 4, C, COLS), F32),
        pltpu.VMEM((GROUPS, 7, ROWS + 6, 16, COLS), BF),
        pltpu.VMEM((ROWS, GROUPS, 16, COLS), F32),
        pltpu.VMEM((C, COLS), F32),
        pltpu.SemaphoreType.DMA((len(args),)),
        pltpu.SemaphoreType.DMA((11 * LAYERS,)),
        pltpu.SemaphoreType.DMA((11 * LAYERS,)),
    ]
    return pl.pallas_call(
        kernel,
        out_shape=jax.ShapeDtypeStruct((C, ROWS, COLS), BF),
        in_specs=[pl.BlockSpec(memory_space=pltpu.HBM)] * len(args),
        out_specs=pl.BlockSpec(memory_space=pltpu.VMEM),
        scratch_shapes=scratch,
        compiler_params=pltpu.CompilerParams(
            collective_id=0, has_side_effects=True, vmem_limit_bytes=40 * 1024 * 1024
        ),
    )(*[pltpu.with_memory_space_constraint(a, pltpu.HBM) for a in args])


def solution(mesh):
    placed = (P(None, "lat", "lon"), P("lat", "lon"), P(), P(), P(), P(), P(), P(), P(), P())
    return jax.shard_map(
        per_device, mesh=mesh, in_specs=placed, out_specs=P(None, "lat", "lon"), check_vma=False
    )
```

```python
import jax
import jax.numpy as jnp
import numpy as np
from jax import lax
from jax.experimental import pallas as pl
from jax.experimental.pallas import tpu as pltpu
from jax.sharding import PartitionSpec as P

LAYERS = 2
C = 96
HID = 384
ROWS = 16
COLS = 128
GROUPS = C // 16
MESH = pl.DeviceIdType.MESH
BF = jnp.bfloat16
F32 = jnp.float32
SIDE = (0, 1, 2, 4, 5, 6)


def ids(shape, dim):
    return lax.broadcasted_iota(jnp.int32, shape, dim)


def kernel(
    field, mask_in, taps_in, dbias_in, gain_in, nbias_in, w_e_in, b_e_in, w_r_in, b_r_in, out,
    raw, mask, taps, dbias, gain, nbias, w_e_raw, b_e, w_r, b_r,
    cells, x_ext, pack, pack_l, pack_r, q_mid, q_halo, mirror, corner, corner_m, halo_t,
    table, w_e, conv_w, tap_w, colv, shifted, mixed, edge, load, send, recv,
):
    lat, lon = lax.axis_index("lat"), lax.axis_index("lon")
    nlat, nlon = lax.axis_size("lat"), lax.axis_size("lon")
    lon_l, lon_r = lax.rem(lon + nlon - 1, nlon), lax.rem(lon + 1, nlon)
    lat_u, lat_d = jnp.minimum(lat + 1, nlat - 1), jnp.maximum(lat - 1, 0)
    fold_r, fold_l = lax.rem(2 * nlon - 2 - lon, nlon), lax.rem(nlon - lon, nlon)
    at_top = lat == nlat - 1
    not_top = lat < nlat - 1
    not_bottom = lat > 0
    fold_r_away = at_top & (fold_r != lon)
    fold_l_away = at_top & (fold_l != lon)
    left = {"lat": lat, "lon": lon_l}
    right = {"lat": lat, "lon": lon_r}
    peers = (
        (left, None), (right, None),
        ({"lat": lat_d, "lon": lon}, not_bottom),
        ({"lat": lat_d, "lon": lon_l}, not_bottom),
        ({"lat": lat_d, "lon": lon_r}, not_bottom),
        ({"lat": lat_u, "lon": lon}, not_top),
        ({"lat": lat_u, "lon": lon_l}, not_top),
        ({"lat": lat_u, "lon": lon_r}, not_top),
        ({"lat": lat, "lon": nlon - 1 - lon}, at_top),
        ({"lat": lat, "lon": fold_r}, fold_r_away),
        ({"lat": lat, "lon": fold_l}, fold_l_away),
    )
    barrier = pltpu.get_barrier_semaphore()

    def when(condition, body):
        if condition is None:
            body()
        else:
            pl.when(condition)(body)

    for device, condition in peers:
        when(
            condition,
            lambda: pl.semaphore_signal(barrier, inc=1, device_id=device, device_id_type=MESH),
        )
    n_peers = sum(1 if c is None else c.astype(jnp.int32) for _, c in peers)

    pairs = (
        (field, raw), (taps_in, taps), (dbias_in, dbias), (gain_in, gain), (nbias_in, nbias), (b_r_in, b_r),
        (w_e_in, w_e_raw), (b_e_in, b_e), (w_r_in, w_r), (mask_in, mask),
    )
    loads = [pltpu.make_async_copy(src, dst, load.at[k]) for k, (src, dst) in enumerate(pairs)]
    for one in loads:
        one.start()

    def remote(src, dst, slot, device):
        return pltpu.make_async_remote_copy(
            src_ref=src, dst_ref=dst, send_sem=send.at[slot], recv_sem=recv.at[slot],
            device_id=device, device_id_type=MESH,
        )

    def copy(layer, k):
        src, dst = (
            (pack.at[layer], pack_r.at[layer]),
            (pack.at[layer], pack_l.at[layer]),
            (x_ext.at[layer, pl.ds(3, 3)], x_ext.at[layer, pl.ds(19, 3)]),
            (corner.at[layer, pl.ds(0, 32)], halo_t.at[layer, 1, pl.ds(0, 32)]),
            (corner.at[layer, pl.ds(0, 32)], halo_t.at[layer, 0, pl.ds(0, 32)]),
            (x_ext.at[layer, pl.ds(16, 3)], x_ext.at[layer, pl.ds(0, 3)]),
            (corner.at[layer, pl.ds(96, 32)], halo_t.at[layer, 1, pl.ds(96, 32)]),
            (corner.at[layer, pl.ds(96, 32)], halo_t.at[layer, 0, pl.ds(96, 32)]),
            (mirror.at[layer], x_ext.at[layer, pl.ds(19, 3)]),
            (corner_m.at[layer], halo_t.at[layer, 1, pl.ds(0, 32)]),
            (corner_m.at[layer], halo_t.at[layer, 0, pl.ds(0, 32)]),
        )[k]
        return remote(src, dst, 11 * layer + k, peers[k][0])

    def start(layer, *numbers):
        for k in numbers:
            when(peers[k][1], lambda: copy(layer, k).start())

    def wait_recv(layer, *numbers):
        for k in numbers:
            condition = {2: not_top, 3: not_top, 4: not_top, 5: not_bottom, 6: not_bottom, 7: not_bottom}.get(k, peers[k][1])
            when(condition, lambda: copy(layer, k).wait_recv())

    def wait_sends(layer):
        for k in range(11):
            when(peers[k][1], lambda: copy(layer, k).wait_send())

    lane = ids((C, COLS), 1)

    def loop(count, body, unroll=1):
        def step(i, carry):
            body(i)
            return carry

        lax.fori_loop(0, count, step, 0, unroll=unroll)

    def add_pack(layer, rows, fresh=False):
        acc = None if fresh else pack[layer]
        for r in rows:
            turned = pltpu.roll(x_ext[layer, 3 + r], 8 * r + 3, axis=1)
            acc = turned if acc is None else jnp.where(lane // 8 == r, turned, acc)
        pack[layer] = acc

    def pick_lanes(rows, total):
        at, lanes = ids((rows, COLS), 0), ids((rows, COLS), 1)
        wanted = at if total is None else (total + COLS - at) % COLS
        return jnp.where(lanes == wanted, 1.0, 0.0).astype(BF)

    def fill_corner(layer):
        wide = jnp.concatenate([pack[layer], jnp.zeros((COLS - C, COLS), BF)], axis=0)

        def pick(rows, total):
            return lax.dot_general(
                pick_lanes(rows, total), wide, (((1,), (1,)), ((), ())), preferred_element_type=F32
            ).astype(BF)

        corner[layer] = pick(COLS, None)

        @pl.when(at_top)
        def _():
            corner_m[layer] = pick(32, 125)

        @pl.when(at_top & (fold_r == lon))
        def _():
            halo_t[layer, 1, 0:32] = corner_m[layer]

        @pl.when(at_top & (fold_l == lon))
        def _():
            halo_t[layer, 0, 0:32] = corner_m[layer]

    def send_low(layer):
        start(layer, 2)

    def send_high(layer):
        start(layer, 5)

        @pl.when(at_top)
        def _():
            flip = jnp.where(ids((COLS, COLS), 0) + ids((COLS, COLS), 1) == COLS - 1, 1.0, 0.0).astype(BF)
            rows = x_ext[layer, 16:19].reshape(3 * C, COLS)
            got = jnp.dot(rows, flip, preferred_element_type=F32).astype(BF)
            for r in range(3):
                mirror[layer, r] = got[(2 - r) * C : (3 - r) * C]
            copy(layer, 8).start()

    def send_pack(layer):
        start(layer, 0, 1)

    def send_corners(layer):
        fill_corner(layer)
        start(layer, 3, 4, 6, 7, 9, 10)

    def take_pack(layer):
        wait_recv(layer, 0, 1)
        q_mid[layer] = jnp.where(lane % 8 >= 3, pack_r[layer], pack_l[layer])

    def take_corners(layer):
        wait_recv(layer, 3, 4, 6, 7, 9, 10)
        at = ids((COLS, COLS), 0)
        low = jnp.where(not_bottom, 96, COLS)
        both = jnp.where(at % 8 >= 3, halo_t[layer, 1].astype(F32), halo_t[layer, 0].astype(F32))
        both = jnp.where((at < 32) | (at >= low), both, 0.0).astype(BF)
        pick = jnp.where(ids((C, COLS), 0) == lane, 1.0, 0.0).astype(BF)
        q_halo[layer] = lax.dot_general(pick, both, (((1,), (1,)), ((), ())), preferred_element_type=F32).astype(BF)

    def take_low(layer):
        wait_recv(layer, 5)

        @pl.when(lat == 0)
        def _():
            x_ext[layer, 0:3] = jnp.zeros((3, C, COLS), BF)

    def take_high(layer):
        wait_recv(layer, 2, 8)

    def build_weights(layer):
        table[...] = jnp.zeros((COLS, COLS), F32)
        table[0:49, 0:C] = taps[:, layer, :]
        for k, v in enumerate((dbias, gain, nbias, b_r)):
            table[49 + k : 50 + k, 0:C] = v[layer : layer + 1, :]
        vec = jnp.transpose(table[...])[0:C]
        for k in range(4):
            colv[layer, k] = jnp.broadcast_to(vec[:, 49 + k : 50 + k], (C, COLS))
        vec = vec.astype(BF)
        bias = b_e[layer : layer + 1, :]
        high = bias.astype(BF).astype(F32)
        wide = jnp.concatenate(
            [w_e_raw[layer].astype(F32), high, bias - high, jnp.zeros((COLS - C - 2, HID), F32)], axis=0
        )
        w_e[layer] = (0.5 * jnp.transpose(wide)).astype(BF)
        shape = (COLS, 7 * COLS)
        at = ids(shape, 1)
        rest = at % COLS
        spread = jnp.where((ids(shape, 0) == (rest // 16) * 7 + at // COLS) & (rest < 112), 1.0, 0.0).astype(BF)
        flat = jnp.dot(vec, spread, preferred_element_type=F32)
        own = (lane % 16) == (ids((C, COLS), 0) % 16)
        zero = jnp.zeros((), BF)
        for d in range(7):
            band = jnp.where(own, flat[:, d * COLS : (d + 1) * COLS], 0.0).astype(BF)
            for r in range(8):
                by = 16 * r
                turned = band if r == 0 else pltpu.roll(band, by, axis=1)
                low = jnp.where(lane >= by, turned, zero)
                high = jnp.where(lane < by, turned, zero)
                at_rows = slice(r * 16, (r + 1) * 16)
                conv_w[layer, :, at_rows, d * 256 : d * 256 + 128] = low.reshape(GROUPS, 16, COLS)
                conv_w[layer, :, at_rows, d * 256 + 128 : d * 256 + 256] = high.reshape(GROUPS, 16, COLS)
        rounded = vec.astype(F32)
        for k in range(49):
            tap_w[layer, k] = jnp.broadcast_to(rounded[:, k : k + 1], (C, COLS))

    def shift_own(layer, r):
        x = x_ext[layer, 3 + r]
        for d in range(-3, 4):
            y = x if d == 0 else pltpu.roll(x, (COLS - d) % COLS, axis=1)
            shifted[:, d + 3, 3 + r] = y.reshape(GROUPS, 16, COLS)

    def conv_own(layer, g):
        x = jnp.concatenate(
            [shifted[g, :, 0:16].reshape(7 * 256, COLS), shifted[g, :, 8:24].reshape(7 * 256, COLS)], axis=1
        )
        got = jnp.dot(conv_w[layer, g], x, preferred_element_type=F32)
        for k in range(2):
            mixed[8 * k : 8 * k + 8, g] = got[:, k * COLS : (k + 1) * COLS].reshape(8, 16, COLS)

    def halo_rows(layer, upper):
        some = lane[0:16]
        for g in range(GROUPS):
            at = slice(16 * g, 16 * g + 16)
            q = q_halo[layer, at].astype(F32)
            total = [jnp.zeros((16, COLS), F32)] * 3
            x, z = [], []
            for k in range(3):
                x.append(x_ext[layer, (19 if upper else 0) + k, at].astype(F32))
                z.append(pltpu.roll(q, 2 * COLS - 3 - 8 * (k if upper else 13 + k), axis=1))
            for d in range(7):
                by = d - 3
                for k in range(3):
                    if by == 0:
                        y = x[k]
                    else:
                        outside = some < by if by > 0 else some >= COLS + by
                        y = pltpu.roll(jnp.where(outside, z[k], x[k]), (COLS - by) % COLS, axis=1)
                    for r in range(3):
                        a = 6 + k - r if upper else k - r
                        if 0 <= a < 7:
                            total[r] = total[r] + tap_w[layer, a * 7 + d, at] * y
            for r in range(3):
                mixed[(13 if upper else 0) + r, g] += total[r]

    def fill_edge(layer):
        delta = q_mid[layer].astype(F32) - pack[layer].astype(F32)
        parts = [jnp.zeros((C, COLS), F32) for _ in SIDE]
        for a in range(7):
            by = 8 * (a - 3)
            if by > 0:
                rows = jnp.where(lane < by, 0.0, delta)
            elif by < 0:
                rows = jnp.where(lane >= COLS + by, 0.0, delta)
            else:
                rows = delta
            for k, d in enumerate(SIDE):
                parts[k] += tap_w[layer, a * 7 + d] * pltpu.roll(rows, (3 * COLS - by - (d - 3)) % COLS, axis=1)
        to = lane % 8
        total = jnp.zeros((C, COLS), F32)
        for part, d in zip(parts, SIDE):
            start = to + d - 3
            if d > 3:
                reach = (to < 3) & (start >= 3) & (start < 6)
            else:
                reach = (to >= 3) & (to < 6) & (start >= 0) & (start < 3)
            total = total + jnp.where(reach, part, 0.0)
        edge[...] = total

    def mlp(layer, at_rows):
        count = len(at_rows)

        def each(pick):
            return jnp.concatenate([pick(r) for r in at_rows], axis=1)

        def same(v):
            return jnp.concatenate([v] * count, axis=1)

        def mixed_row(r):
            beside = pltpu.roll(edge[...], (2 * COLS - 3 - 8 * r) % COLS, axis=1)
            return mixed[r].reshape(C, COLS) + jnp.where((lane < 3) | (lane >= COLS - 3), beside, 0.0)

        c = each(mixed_row) + same(colv[layer, 0])
        mean = jnp.sum(c, axis=0, keepdims=True) * (1.0 / C)
        c = c - mean
        var = jnp.sum(c * c, axis=0, keepdims=True) * (1.0 / C)
        n = c * lax.rsqrt(var + 1e-6) * same(colv[layer, 1]) + same(colv[layer, 2])
        ones = jnp.where(ids((32, count * COLS), 0) < 2, 1.0, 0.0)
        n = jnp.concatenate([n, ones], axis=0).astype(BF)
        half = jnp.dot(w_e[layer], n, preferred_element_type=F32)
        h = (half + half * lax.erf(half * np.float32(np.sqrt(2.0)))).astype(BF)
        u = jnp.dot(w_r[layer], h, preferred_element_type=F32) + same(colv[layer, 3])
        x = each(lambda r: x_ext[layer, 3 + r]).astype(F32)
        flags = each(lambda r: mask[r : r + 1, :]).astype(F32)
        y = flags * (x + u)
        for k, r in enumerate(at_rows):
            part = y[:, k * COLS : (k + 1) * COLS]
            if layer == LAYERS - 1:
                cells[pl.ds(r, C, stride=ROWS), :] = part
            else:
                x_ext[layer + 1, 3 + r] = part.astype(BF)

    loads[0].wait()
    cells[...] = raw[...].astype(F32).reshape(C * ROWS, COLS)
    for r in range(ROWS):
        x_ext[0, 3 + r] = cells[pl.ds(r, C, stride=ROWS), :].astype(BF)
    add_pack(0, range(ROWS), fresh=True)
    for rows in (slice(0, 3), slice(19, 24)):
        shifted[:, :, rows] = jnp.zeros((GROUPS, 7, rows.stop - rows.start, 16, COLS), BF)
    pl.semaphore_wait(barrier, n_peers)
    send_low(0)
    send_high(0)
    send_pack(0)
    send_corners(0)
    for one in loads[1:]:
        one.wait()
    build_weights(0)

    def interior(layer):
        for r in range(3, 13, 2):
            mlp(layer, (r, r + 1))

    for layer in range(LAYERS):
        onward = layer + 1 < LAYERS
        loop(ROWS, lambda r: shift_own(layer, r), ROWS)
        loop(GROUPS, lambda g: conv_own(layer, g), GROUPS)
        take_pack(layer)
        fill_edge(layer)
        if onward:
            build_weights(layer + 1)
        else:
            interior(layer)
        take_corners(layer)
        take_low(layer)
        halo_rows(layer, False)
        mlp(layer, (0, 1, 2))
        if onward:
            send_low(layer + 1)
        take_high(layer)
        halo_rows(layer, True)
        mlp(layer, (13, 14, 15))
        if onward:
            send_high(layer + 1)
            add_pack(layer + 1, (0, 1, 2, 13, 14, 15), fresh=True)
            send_corners(layer + 1)
            interior(layer)
            add_pack(layer + 1, range(3, 13))
            send_pack(layer + 1)
    out[...] = cells[...].reshape(C, ROWS, COLS).astype(BF)
    for layer in range(LAYERS):
        wait_sends(layer)


def per_device(
    field, land_mask, depth_kernel, depth_bias, norm_gain, norm_bias, w_expand, b_expand, w_reduce, b_reduce
):
    taps = jnp.transpose(depth_kernel, (2, 3, 0, 1)).reshape(49, LAYERS, C)
    args = (
        field, land_mask, taps, depth_bias, norm_gain, norm_bias, jnp.transpose(w_expand, (0, 2, 1)), b_expand,
        w_reduce, b_reduce,
    )
    tile = (LAYERS, C, COLS)
    held = [pltpu.VMEM(a.shape, a.dtype) for a in args]
    scratch = held + [
        pltpu.VMEM((C * ROWS, COLS), F32),
        pltpu.VMEM((LAYERS, ROWS + 6, C, COLS), BF),
    ]
    scratch += [pltpu.VMEM(tile, BF)] * 5
    scratch += [
        pltpu.VMEM((LAYERS, 3, C, COLS), BF),
        pltpu.VMEM((LAYERS, COLS, COLS), BF),
        pltpu.VMEM((LAYERS, 32, COLS), BF),
        pltpu.VMEM((LAYERS, 2, COLS, COLS), BF),
        pltpu.VMEM((COLS, COLS), F32),
        pltpu.VMEM((LAYERS, HID, COLS), BF),
        pltpu.VMEM((LAYERS, GROUPS, COLS, 7 * 256), BF),
        pltpu.VMEM((LAYERS, 49, C, COLS), F32),
        pltpu.VMEM((LAYERS, 4, C, COLS), F32),
        pltpu.VMEM((GROUPS, 7, ROWS + 8, 16, COLS), BF),
        pltpu.VMEM((ROWS, GROUPS, 16, COLS), F32),
        pltpu.VMEM((C, COLS), F32),
        pltpu.SemaphoreType.DMA((len(args),)),
        pltpu.SemaphoreType.DMA((11 * LAYERS,)),
        pltpu.SemaphoreType.DMA((11 * LAYERS,)),
    ]
    return pl.pallas_call(
        kernel,
        out_shape=jax.ShapeDtypeStruct((C, ROWS, COLS), BF),
        in_specs=[pl.BlockSpec(memory_space=pltpu.HBM)] * len(args),
        out_specs=pl.BlockSpec(memory_space=pltpu.VMEM),
        scratch_shapes=scratch,
        compiler_params=pltpu.CompilerParams(
            collective_id=0, has_side_effects=True, vmem_limit_bytes=40 * 1024 * 1024
        ),
    )(*[pltpu.with_memory_space_constraint(a, pltpu.HBM) for a in args])


def solution(mesh):
    placed = (P(None, "lat", "lon"), P("lat", "lon"), P(), P(), P(), P(), P(), P(), P(), P())
    return jax.shard_map(
        per_device, mesh=mesh, in_specs=placed, out_specs=P(None, "lat", "lon"), check_vma=False
    )
```

```python
import jax
import jax.numpy as jnp
import numpy as np
from jax import lax
from jax.experimental import pallas as pl
from jax.experimental.pallas import tpu as pltpu
from jax.sharding import PartitionSpec as P

LAYERS = 2
C = 96
HID = 384
ROWS = 16
COLS = 128
GROUPS = C // 16
MESH = pl.DeviceIdType.MESH
BF = jnp.bfloat16
F32 = jnp.float32
SIDE = (0, 1, 2, 4, 5, 6)


def ids(shape, dim):
    return lax.broadcasted_iota(jnp.int32, shape, dim)


def kernel(
    field, mask_in, taps_in, dbias_in, gain_in, nbias_in, w_e_in, b_e_in, w_r_in, b_r_in, out,
    raw, mask, taps, dbias, gain, nbias, w_e_raw, b_e, w_r, b_r,
    cells, x_ext, pack, pack_l, pack_r, q_mid, q_halo, mirror, corner, corner_m, halo_t,
    table, w_e, conv_w, tap_w, colv, shifted, mixed, edge, load, send, recv,
):
    lat, lon = lax.axis_index("lat"), lax.axis_index("lon")
    nlat, nlon = lax.axis_size("lat"), lax.axis_size("lon")
    lon_l, lon_r = lax.rem(lon + nlon - 1, nlon), lax.rem(lon + 1, nlon)
    lat_u, lat_d = jnp.minimum(lat + 1, nlat - 1), jnp.maximum(lat - 1, 0)
    fold_r, fold_l = lax.rem(2 * nlon - 2 - lon, nlon), lax.rem(nlon - lon, nlon)
    at_top = lat == nlat - 1
    not_top = lat < nlat - 1
    not_bottom = lat > 0
    fold_r_away = at_top & (fold_r != lon)
    fold_l_away = at_top & (fold_l != lon)
    left = {"lat": lat, "lon": lon_l}
    right = {"lat": lat, "lon": lon_r}
    peers = (
        (left, None), (right, None),
        ({"lat": lat_d, "lon": lon}, not_bottom),
        ({"lat": lat_d, "lon": lon_l}, not_bottom),
        ({"lat": lat_d, "lon": lon_r}, not_bottom),
        ({"lat": lat_u, "lon": lon}, not_top),
        ({"lat": lat_u, "lon": lon_l}, not_top),
        ({"lat": lat_u, "lon": lon_r}, not_top),
        ({"lat": lat, "lon": nlon - 1 - lon}, at_top),
        ({"lat": lat, "lon": fold_r}, fold_r_away),
        ({"lat": lat, "lon": fold_l}, fold_l_away),
    )
    barrier = pltpu.get_barrier_semaphore()

    def when(condition, body):
        if condition is None:
            body()
        else:
            pl.when(condition)(body)

    for device, condition in peers:
        when(
            condition,
            lambda: pl.semaphore_signal(barrier, inc=1, device_id=device, device_id_type=MESH),
        )
    n_peers = sum(1 if c is None else c.astype(jnp.int32) for _, c in peers)

    pairs = (
        (field, raw), (taps_in, taps), (dbias_in, dbias), (gain_in, gain), (nbias_in, nbias), (b_r_in, b_r),
        (w_e_in, w_e_raw), (b_e_in, b_e), (w_r_in, w_r), (mask_in, mask),
    )
    loads = [pltpu.make_async_copy(src, dst, load.at[k]) for k, (src, dst) in enumerate(pairs)]
    for one in loads:
        one.start()

    def remote(src, dst, slot, device):
        return pltpu.make_async_remote_copy(
            src_ref=src, dst_ref=dst, send_sem=send.at[slot], recv_sem=recv.at[slot],
            device_id=device, device_id_type=MESH,
        )

    def copy(layer, k):
        src, dst = (
            (pack.at[layer], pack_r.at[layer]),
            (pack.at[layer], pack_l.at[layer]),
            (x_ext.at[layer, pl.ds(3, 3)], x_ext.at[layer, pl.ds(19, 3)]),
            (corner.at[layer, pl.ds(0, 32)], halo_t.at[layer, 1, pl.ds(0, 32)]),
            (corner.at[layer, pl.ds(0, 32)], halo_t.at[layer, 0, pl.ds(0, 32)]),
            (x_ext.at[layer, pl.ds(16, 3)], x_ext.at[layer, pl.ds(0, 3)]),
            (corner.at[layer, pl.ds(96, 32)], halo_t.at[layer, 1, pl.ds(96, 32)]),
            (corner.at[layer, pl.ds(96, 32)], halo_t.at[layer, 0, pl.ds(96, 32)]),
            (mirror.at[layer], x_ext.at[layer, pl.ds(19, 3)]),
            (corner_m.at[layer], halo_t.at[layer, 1, pl.ds(0, 32)]),
            (corner_m.at[layer], halo_t.at[layer, 0, pl.ds(0, 32)]),
        )[k]
        return remote(src, dst, 11 * layer + k, peers[k][0])

    def start(layer, *numbers):
        for k in numbers:
            when(peers[k][1], lambda: copy(layer, k).start())

    def wait_recv(layer, *numbers):
        for k in numbers:
            condition = {2: not_top, 3: not_top, 4: not_top, 5: not_bottom, 6: not_bottom, 7: not_bottom}.get(k, peers[k][1])
            when(condition, lambda: copy(layer, k).wait_recv())

    def wait_sends(layer):
        for k in range(11):
            when(peers[k][1], lambda: copy(layer, k).wait_send())

    lane = ids((C, COLS), 1)

    def loop(count, body, unroll=1):
        def step(i, carry):
            body(i)
            return carry

        lax.fori_loop(0, count, step, 0, unroll=unroll)

    def add_pack(layer, rows, fresh=False):
        acc = None if fresh else pack[layer]
        for r in rows:
            turned = pltpu.roll(x_ext[layer, 3 + r], 8 * r + 3, axis=1)
            acc = turned if acc is None else jnp.where(lane // 8 == r, turned, acc)
        pack[layer] = acc

    def pick_lanes(rows, total):
        at, lanes = ids((rows, COLS), 0), ids((rows, COLS), 1)
        wanted = at if total is None else (total + COLS - at) % COLS
        return jnp.where(lanes == wanted, 1.0, 0.0).astype(BF)

    def fill_corner(layer):
        wide = jnp.concatenate([pack[layer], jnp.zeros((COLS - C, COLS), BF)], axis=0)

        def pick(rows, total):
            return lax.dot_general(
                pick_lanes(rows, total), wide, (((1,), (1,)), ((), ())), preferred_element_type=F32
            ).astype(BF)

        corner[layer] = pick(COLS, None)

        @pl.when(at_top)
        def _():
            corner_m[layer] = pick(32, 125)

        @pl.when(at_top & (fold_r == lon))
        def _():
            halo_t[layer, 1, 0:32] = corner_m[layer]

        @pl.when(at_top & (fold_l == lon))
        def _():
            halo_t[layer, 0, 0:32] = corner_m[layer]

    def send_low(layer):
        start(layer, 2)

    def fill_mirror(layer):
        @pl.when(at_top)
        def _():
            flip = jnp.where(ids((COLS, COLS), 0) + ids((COLS, COLS), 1) == COLS - 1, 1.0, 0.0).astype(BF)
            rows = x_ext[layer, 16:19].reshape(3 * C, COLS)
            got = jnp.dot(rows, flip, preferred_element_type=F32).astype(BF)
            for r in range(3):
                mirror[layer, r] = got[(2 - r) * C : (3 - r) * C]

    def send_high(layer):
        start(layer, 5, 8)

    def send_pack(layer):
        start(layer, 0, 1)

    def send_corners(layer):
        fill_corner(layer)
        start(layer, 3, 4, 6, 7, 9, 10)

    def take_pack(layer):
        wait_recv(layer, 0, 1)
        q_mid[layer] = jnp.where(lane % 8 >= 3, pack_r[layer], pack_l[layer])

    def take_corners(layer):
        wait_recv(layer, 3, 4, 6, 7, 9, 10)
        at = ids((COLS, COLS), 0)
        low = jnp.where(not_bottom, 96, COLS)
        both = jnp.where(at % 8 >= 3, halo_t[layer, 1].astype(F32), halo_t[layer, 0].astype(F32))
        both = jnp.where((at < 32) | (at >= low), both, 0.0).astype(BF)
        pick = jnp.where(ids((C, COLS), 0) == lane, 1.0, 0.0).astype(BF)
        q_halo[layer] = lax.dot_general(pick, both, (((1,), (1,)), ((), ())), preferred_element_type=F32).astype(BF)

    def take_low(layer):
        wait_recv(layer, 5)

        @pl.when(lat == 0)
        def _():
            x_ext[layer, 0:3] = jnp.zeros((3, C, COLS), BF)

    def take_high(layer):
        wait_recv(layer, 2, 8)

    def build_weights(layer):
        table[...] = jnp.zeros((COLS, COLS), F32)
        table[0:49, 0:C] = taps[:, layer, :]
        for k, v in enumerate((dbias, gain, nbias, b_r)):
            table[49 + k : 50 + k, 0:C] = v[layer : layer + 1, :]
        vec = jnp.transpose(table[...])[0:C]
        for k in range(4):
            colv[layer, k] = jnp.broadcast_to(vec[:, 49 + k : 50 + k], (C, COLS))
        vec = vec.astype(BF)
        bias = b_e[layer : layer + 1, :]
        high = bias.astype(BF).astype(F32)
        wide = jnp.concatenate(
            [w_e_raw[layer].astype(F32), high, bias - high, jnp.zeros((COLS - C - 2, HID), F32)], axis=0
        )
        w_e[layer] = (0.5 * jnp.transpose(wide)).astype(BF)
        shape = (COLS, 7 * COLS)
        at = ids(shape, 1)
        rest = at % COLS
        spread = jnp.where((ids(shape, 0) == (rest // 16) * 7 + at // COLS) & (rest < 112), 1.0, 0.0).astype(BF)
        flat = jnp.dot(vec, spread, preferred_element_type=F32)
        own = (lane % 16) == (ids((C, COLS), 0) % 16)
        zero = jnp.zeros((), BF)
        for d in range(7):
            band = jnp.where(own, flat[:, d * COLS : (d + 1) * COLS], 0.0).astype(BF)
            for r in range(8):
                by = 16 * r
                turned = band if r == 0 else pltpu.roll(band, by, axis=1)
                low = jnp.where(lane >= by, turned, zero)
                high = jnp.where(lane < by, turned, zero)
                at_rows = slice(r * 16, (r + 1) * 16)
                conv_w[layer, :, at_rows, d * 256 : d * 256 + 128] = low.reshape(GROUPS, 16, COLS)
                conv_w[layer, :, at_rows, d * 256 + 128 : d * 256 + 256] = high.reshape(GROUPS, 16, COLS)
        rounded = vec.astype(F32)
        for k in range(49):
            tap_w[layer, k] = jnp.broadcast_to(rounded[:, k : k + 1], (C, COLS))

    def shift_own(layer, r):
        x = x_ext[layer, 3 + r]
        for d in range(-3, 4):
            y = x if d == 0 else pltpu.roll(x, (COLS - d) % COLS, axis=1)
            shifted[:, d + 3, 3 + r] = y.reshape(GROUPS, 16, COLS)

    def conv_own(layer, g):
        x = jnp.concatenate(
            [shifted[g, :, 0:16].reshape(7 * 256, COLS), shifted[g, :, 8:24].reshape(7 * 256, COLS)], axis=1
        )
        got = jnp.dot(conv_w[layer, g], x, preferred_element_type=F32)
        for k in range(2):
            mixed[8 * k : 8 * k + 8, g] = got[:, k * COLS : (k + 1) * COLS].reshape(8, 16, COLS)

    def halo_rows(layer, upper):
        some = lane[0:16]
        for g in range(GROUPS):
            at = slice(16 * g, 16 * g + 16)
            q = q_halo[layer, at].astype(F32)
            total = [jnp.zeros((16, COLS), F32)] * 3
            x, z = [], []
            for k in range(3):
                x.append(x_ext[layer, (19 if upper else 0) + k, at].astype(F32))
                z.append(pltpu.roll(q, 2 * COLS - 3 - 8 * (k if upper else 13 + k), axis=1))
            for d in range(7):
                by = d - 3
                for k in range(3):
                    if by == 0:
                        y = x[k]
                    else:
                        outside = some < by if by > 0 else some >= COLS + by
                        y = pltpu.roll(jnp.where(outside, z[k], x[k]), (COLS - by) % COLS, axis=1)
                    for r in range(3):
                        a = 6 + k - r if upper else k - r
                        if 0 <= a < 7:
                            total[r] = total[r] + tap_w[layer, a * 7 + d, at] * y
            for r in range(3):
                mixed[(13 if upper else 0) + r, g] += total[r]

    def fill_edge(layer):
        delta = q_mid[layer].astype(F32) - pack[layer].astype(F32)
        parts = [jnp.zeros((C, COLS), F32) for _ in SIDE]
        for a in range(7):
            by = 8 * (a - 3)
            if by > 0:
                rows = jnp.where(lane < by, 0.0, delta)
            elif by < 0:
                rows = jnp.where(lane >= COLS + by, 0.0, delta)
            else:
                rows = delta
            for k, d in enumerate(SIDE):
                parts[k] += tap_w[layer, a * 7 + d] * pltpu.roll(rows, (3 * COLS - by - (d - 3)) % COLS, axis=1)
        to = lane % 8
        total = jnp.zeros((C, COLS), F32)
        for part, d in zip(parts, SIDE):
            start = to + d - 3
            if d > 3:
                reach = (to < 3) & (start >= 3) & (start < 6)
            else:
                reach = (to >= 3) & (to < 6) & (start >= 0) & (start < 3)
            total = total + jnp.where(reach, part, 0.0)
        edge[...] = total

    def mlp(layer, at_rows):
        count = len(at_rows)

        def each(pick):
            return jnp.concatenate([pick(r) for r in at_rows], axis=1)

        def same(v):
            return jnp.concatenate([v] * count, axis=1)

        def mixed_row(r):
            beside = pltpu.roll(edge[...], (2 * COLS - 3 - 8 * r) % COLS, axis=1)
            return mixed[r].reshape(C, COLS) + jnp.where((lane < 3) | (lane >= COLS - 3), beside, 0.0)

        c = each(mixed_row) + same(colv[layer, 0])
        mean = jnp.sum(c, axis=0, keepdims=True) * (1.0 / C)
        c = c - mean
        var = jnp.sum(c * c, axis=0, keepdims=True) * (1.0 / C)
        n = c * lax.rsqrt(var + 1e-6) * same(colv[layer, 1]) + same(colv[layer, 2])
        ones = jnp.where(ids((32, count * COLS), 0) < 2, 1.0, 0.0)
        n = jnp.concatenate([n, ones], axis=0).astype(BF)
        half = jnp.dot(w_e[layer], n, preferred_element_type=F32)
        h = (half + half * lax.erf(half * np.float32(np.sqrt(2.0)))).astype(BF)
        u = jnp.dot(w_r[layer], h, preferred_element_type=F32) + same(colv[layer, 3])
        x = each(lambda r: x_ext[layer, 3 + r]).astype(F32)
        flags = each(lambda r: mask[r : r + 1, :]).astype(F32)
        y = flags * (x + u)
        for k, r in enumerate(at_rows):
            part = y[:, k * COLS : (k + 1) * COLS]
            if layer == LAYERS - 1:
                cells[pl.ds(r, C, stride=ROWS), :] = part
            else:
                x_ext[layer + 1, 3 + r] = part.astype(BF)

    loads[0].wait()
    cells[...] = raw[...].astype(F32).reshape(C * ROWS, COLS)

    def take_rows(rows):
        for r in rows:
            x_ext[0, 3 + r] = cells[pl.ds(r, C, stride=ROWS), :].astype(BF)

    take_rows((0, 1, 2, 13, 14, 15))
    fill_mirror(0)
    take_rows(range(3, 13))
    add_pack(0, range(ROWS), fresh=True)
    pl.semaphore_wait(barrier, n_peers)
    send_pack(0)
    send_high(0)
    send_low(0)
    send_corners(0)
    for rows in (slice(0, 3), slice(19, 24)):
        shifted[:, :, rows] = jnp.zeros((GROUPS, 7, rows.stop - rows.start, 16, COLS), BF)
    for one in loads[1:]:
        one.wait()
    build_weights(0)

    def interior(layer):
        for r in range(3, 13, 2):
            mlp(layer, (r, r + 1))

    for layer in range(LAYERS):
        onward = layer + 1 < LAYERS
        loop(ROWS, lambda r: shift_own(layer, r), ROWS)
        loop(GROUPS, lambda g: conv_own(layer, g), GROUPS)
        take_pack(layer)
        fill_edge(layer)
        interior(layer)
        if onward:
            add_pack(layer + 1, range(3, 13), fresh=True)
        take_corners(layer)
        take_low(layer)
        take_high(layer)
        halo_rows(layer, False)
        halo_rows(layer, True)
        mlp(layer, (0, 1, 2))
        mlp(layer, (13, 14, 15))
        if onward:
            fill_mirror(layer + 1)
            add_pack(layer + 1, (0, 1, 2, 13, 14, 15))
            send_pack(layer + 1)
            send_high(layer + 1)
            send_low(layer + 1)
            send_corners(layer + 1)
            build_weights(layer + 1)
    out[...] = cells[...].reshape(C, ROWS, COLS).astype(BF)
    for layer in range(LAYERS):
        wait_sends(layer)


def per_device(
    field, land_mask, depth_kernel, depth_bias, norm_gain, norm_bias, w_expand, b_expand, w_reduce, b_reduce
):
    taps = jnp.transpose(depth_kernel, (2, 3, 0, 1)).reshape(49, LAYERS, C)
    args = (
        field, land_mask, taps, depth_bias, norm_gain, norm_bias, jnp.transpose(w_expand, (0, 2, 1)), b_expand,
        w_reduce, b_reduce,
    )
    tile = (LAYERS, C, COLS)
    held = [pltpu.VMEM(a.shape, a.dtype) for a in args]
    scratch = held + [
        pltpu.VMEM((C * ROWS, COLS), F32),
        pltpu.VMEM((LAYERS, ROWS + 6, C, COLS), BF),
    ]
    scratch += [pltpu.VMEM(tile, BF)] * 5
    scratch += [
        pltpu.VMEM((LAYERS, 3, C, COLS), BF),
        pltpu.VMEM((LAYERS, COLS, COLS), BF),
        pltpu.VMEM((LAYERS, 32, COLS), BF),
        pltpu.VMEM((LAYERS, 2, COLS, COLS), BF),
        pltpu.VMEM((COLS, COLS), F32),
        pltpu.VMEM((LAYERS, HID, COLS), BF),
        pltpu.VMEM((LAYERS, GROUPS, COLS, 7 * 256), BF),
        pltpu.VMEM((LAYERS, 49, C, COLS), F32),
        pltpu.VMEM((LAYERS, 4, C, COLS), F32),
        pltpu.VMEM((GROUPS, 7, ROWS + 8, 16, COLS), BF),
        pltpu.VMEM((ROWS, GROUPS, 16, COLS), F32),
        pltpu.VMEM((C, COLS), F32),
        pltpu.SemaphoreType.DMA((len(args),)),
        pltpu.SemaphoreType.DMA((11 * LAYERS,)),
        pltpu.SemaphoreType.DMA((11 * LAYERS,)),
    ]
    return pl.pallas_call(
        kernel,
        out_shape=jax.ShapeDtypeStruct((C, ROWS, COLS), BF),
        in_specs=[pl.BlockSpec(memory_space=pltpu.HBM)] * len(args),
        out_specs=pl.BlockSpec(memory_space=pltpu.VMEM),
        scratch_shapes=scratch,
        compiler_params=pltpu.CompilerParams(
            collective_id=0, has_side_effects=True, vmem_limit_bytes=40 * 1024 * 1024
        ),
    )(*[pltpu.with_memory_space_constraint(a, pltpu.HBM) for a in args])


def solution(mesh):
    placed = (P(None, "lat", "lon"), P("lat", "lon"), P(), P(), P(), P(), P(), P(), P(), P())
    return jax.shard_map(
        per_device, mesh=mesh, in_specs=placed, out_specs=P(None, "lat", "lon"), check_vma=False
    )
```

```python
import jax
import jax.numpy as jnp
import numpy as np
from jax import lax
from jax.experimental import pallas as pl
from jax.experimental.pallas import tpu as pltpu
from jax.sharding import PartitionSpec as P

LAYERS = 2
C = 96
HID = 384
ROWS = 16
COLS = 128
GROUPS = C // 16
MESH = pl.DeviceIdType.MESH
BF = jnp.bfloat16
F32 = jnp.float32
SIDE = (0, 1, 2, 4, 5, 6)


def ids(shape, dim):
    return lax.broadcasted_iota(jnp.int32, shape, dim)


def kernel(
    field, mask_in, taps_in, dbias_in, gain_in, nbias_in, w_e_in, b_e_in, w_r_in, b_r_in, out,
    raw, mask, taps, dbias, gain, nbias, w_e_raw, b_e, w_r, b_r,
    cells, x_ext, pack, pack_l, pack_r, q_mid, q_halo, mirror, corner, corner_m, halo_t,
    table, w_e, conv_w, tap_w, colv, shifted, mixed, edge, load, send, recv,
):
    lat, lon = lax.axis_index("lat"), lax.axis_index("lon")
    nlat, nlon = lax.axis_size("lat"), lax.axis_size("lon")
    lon_l, lon_r = lax.rem(lon + nlon - 1, nlon), lax.rem(lon + 1, nlon)
    lat_u, lat_d = jnp.minimum(lat + 1, nlat - 1), jnp.maximum(lat - 1, 0)
    fold_r, fold_l = lax.rem(2 * nlon - 2 - lon, nlon), lax.rem(nlon - lon, nlon)
    at_top = lat == nlat - 1
    not_top = lat < nlat - 1
    not_bottom = lat > 0
    fold_r_away = at_top & (fold_r != lon)
    fold_l_away = at_top & (fold_l != lon)
    left = {"lat": lat, "lon": lon_l}
    right = {"lat": lat, "lon": lon_r}
    peers = (
        (left, None), (right, None),
        ({"lat": lat_d, "lon": lon}, not_bottom),
        ({"lat": lat_d, "lon": lon_l}, not_bottom),
        ({"lat": lat_d, "lon": lon_r}, not_bottom),
        ({"lat": lat_u, "lon": lon}, not_top),
        ({"lat": lat_u, "lon": lon_l}, not_top),
        ({"lat": lat_u, "lon": lon_r}, not_top),
        ({"lat": lat, "lon": nlon - 1 - lon}, at_top),
        ({"lat": lat, "lon": fold_r}, fold_r_away),
        ({"lat": lat, "lon": fold_l}, fold_l_away),
    )
    barrier = pltpu.get_barrier_semaphore()

    def when(condition, body):
        if condition is None:
            body()
        else:
            pl.when(condition)(body)

    for device, condition in peers:
        when(
            condition,
            lambda: pl.semaphore_signal(barrier, inc=1, device_id=device, device_id_type=MESH),
        )
    n_peers = sum(1 if c is None else c.astype(jnp.int32) for _, c in peers)

    pairs = (
        (field, raw), (taps_in, taps), (dbias_in, dbias), (gain_in, gain), (nbias_in, nbias), (b_r_in, b_r),
        (w_e_in, w_e_raw), (b_e_in, b_e), (w_r_in, w_r), (mask_in, mask),
    )
    loads = [pltpu.make_async_copy(src, dst, load.at[k]) for k, (src, dst) in enumerate(pairs)]
    for one in loads:
        one.start()

    def remote(src, dst, slot, device):
        return pltpu.make_async_remote_copy(
            src_ref=src, dst_ref=dst, send_sem=send.at[slot], recv_sem=recv.at[slot],
            device_id=device, device_id_type=MESH,
        )

    def copy(layer, k):
        src, dst = (
            (pack.at[layer], pack_r.at[layer]),
            (pack.at[layer], pack_l.at[layer]),
            (x_ext.at[layer, pl.ds(3, 3)], x_ext.at[layer, pl.ds(19, 3)]),
            (corner.at[layer, pl.ds(0, 32)], halo_t.at[layer, 1, pl.ds(0, 32)]),
            (corner.at[layer, pl.ds(0, 32)], halo_t.at[layer, 0, pl.ds(0, 32)]),
            (x_ext.at[layer, pl.ds(16, 3)], x_ext.at[layer, pl.ds(0, 3)]),
            (corner.at[layer, pl.ds(96, 32)], halo_t.at[layer, 1, pl.ds(96, 32)]),
            (corner.at[layer, pl.ds(96, 32)], halo_t.at[layer, 0, pl.ds(96, 32)]),
            (mirror.at[layer], x_ext.at[layer, pl.ds(19, 3)]),
            (corner_m.at[layer], halo_t.at[layer, 1, pl.ds(0, 32)]),
            (corner_m.at[layer], halo_t.at[layer, 0, pl.ds(0, 32)]),
        )[k]
        return remote(src, dst, 11 * layer + k, peers[k][0])

    def start(layer, *numbers):
        for k in numbers:
            when(peers[k][1], lambda: copy(layer, k).start())

    def wait_recv(layer, *numbers):
        for k in numbers:
            condition = {2: not_top, 3: not_top, 4: not_top, 5: not_bottom, 6: not_bottom, 7: not_bottom}.get(k, peers[k][1])
            when(condition, lambda: copy(layer, k).wait_recv())

    def wait_sends(layer):
        for k in range(11):
            when(peers[k][1], lambda: copy(layer, k).wait_send())

    lane = ids((C, COLS), 1)

    def loop(count, body, unroll=1):
        def step(i, carry):
            body(i)
            return carry

        lax.fori_loop(0, count, step, 0, unroll=unroll)

    def add_pack(layer, rows, fresh=False):
        acc = None if fresh else pack[layer]
        for r in rows:
            turned = pltpu.roll(x_ext[layer, 3 + r], 8 * r + 3, axis=1)
            acc = turned if acc is None else jnp.where(lane // 8 == r, turned, acc)
        pack[layer] = acc

    def pick_lanes(rows, total):
        at, lanes = ids((rows, COLS), 0), ids((rows, COLS), 1)
        wanted = at if total is None else (total + COLS - at) % COLS
        return jnp.where(lanes == wanted, 1.0, 0.0).astype(BF)

    def fill_corner(layer):
        wide = jnp.concatenate([pack[layer], jnp.zeros((COLS - C, COLS), BF)], axis=0)

        def pick(rows, total):
            return lax.dot_general(
                pick_lanes(rows, total), wide, (((1,), (1,)), ((), ())), preferred_element_type=F32
            ).astype(BF)

        corner[layer] = pick(COLS, None)

        @pl.when(at_top)
        def _():
            corner_m[layer] = pick(32, 125)

        @pl.when(at_top & (fold_r == lon))
        def _():
            halo_t[layer, 1, 0:32] = corner_m[layer]

        @pl.when(at_top & (fold_l == lon))
        def _():
            halo_t[layer, 0, 0:32] = corner_m[layer]

    def send_low(layer):
        start(layer, 2)

    def fill_mirror(layer):
        @pl.when(at_top)
        def _():
            flip = jnp.where(ids((COLS, COLS), 0) + ids((COLS, COLS), 1) == COLS - 1, 1.0, 0.0).astype(BF)
            rows = x_ext[layer, 16:19].reshape(3 * C, COLS)
            got = jnp.dot(rows, flip, preferred_element_type=F32).astype(BF)
            for r in range(3):
                mirror[layer, r] = got[(2 - r) * C : (3 - r) * C]

    def send_high(layer):
        start(layer, 5, 8)

    def send_pack(layer):
        start(layer, 0, 1)

    def send_corners(layer):
        fill_corner(layer)
        start(layer, 3, 4, 6, 7, 9, 10)

    def take_pack(layer):
        wait_recv(layer, 0, 1)
        q_mid[layer] = jnp.where(lane % 8 >= 3, pack_r[layer], pack_l[layer])

    def take_corners(layer):
        wait_recv(layer, 3, 4, 6, 7, 9, 10)
        at = ids((COLS, COLS), 0)
        low = jnp.where(not_bottom, 96, COLS)
        both = jnp.where(at % 8 >= 3, halo_t[layer, 1].astype(F32), halo_t[layer, 0].astype(F32))
        both = jnp.where((at < 32) | (at >= low), both, 0.0).astype(BF)
        pick = jnp.where(ids((C, COLS), 0) == lane, 1.0, 0.0).astype(BF)
        q_halo[layer] = lax.dot_general(pick, both, (((1,), (1,)), ((), ())), preferred_element_type=F32).astype(BF)

    def take_low(layer):
        wait_recv(layer, 5)

        @pl.when(lat == 0)
        def _():
            x_ext[layer, 0:3] = jnp.zeros((3, C, COLS), BF)

    def take_high(layer):
        wait_recv(layer, 2, 8)

    def build_weights(layer):
        table[...] = jnp.zeros((COLS, COLS), F32)
        table[0:49, 0:C] = taps[:, layer, :]
        for k, v in enumerate((dbias, gain, nbias, b_r)):
            table[49 + k : 50 + k, 0:C] = v[layer : layer + 1, :]
        vec = jnp.transpose(table[...])[0:C]
        for k in range(4):
            colv[layer, k] = jnp.broadcast_to(vec[:, 49 + k : 50 + k], (C, COLS))
        vec = vec.astype(BF)
        bias = b_e[layer : layer + 1, :]
        high = bias.astype(BF).astype(F32)
        wide = jnp.concatenate(
            [w_e_raw[layer].astype(F32), high, bias - high, jnp.zeros((COLS - C - 2, HID), F32)], axis=0
        )
        w_e[layer] = (0.5 * jnp.transpose(wide)).astype(BF)
        shape = (COLS, 7 * COLS)
        at = ids(shape, 1)
        rest = at % COLS
        spread = jnp.where((ids(shape, 0) == (rest // 16) * 7 + at // COLS) & (rest < 112), 1.0, 0.0).astype(BF)
        flat = jnp.dot(vec, spread, preferred_element_type=F32)
        own = (lane % 16) == (ids((C, COLS), 0) % 16)
        zero = jnp.zeros((), BF)
        for d in range(7):
            band = jnp.where(own, flat[:, d * COLS : (d + 1) * COLS], 0.0).astype(BF)
            for r in range(8):
                by = 16 * r
                turned = band if r == 0 else pltpu.roll(band, by, axis=1)
                low = jnp.where(lane >= by, turned, zero)
                high = jnp.where(lane < by, turned, zero)
                at_rows = slice(r * 16, (r + 1) * 16)
                conv_w[layer, :, at_rows, d * 256 : d * 256 + 128] = low.reshape(GROUPS, 16, COLS)
                conv_w[layer, :, at_rows, d * 256 + 128 : d * 256 + 256] = high.reshape(GROUPS, 16, COLS)
        rounded = vec.astype(F32)
        for k in range(49):
            tap_w[layer, k] = jnp.broadcast_to(rounded[:, k : k + 1], (C, COLS))

    def shift_own(layer, r):
        x = x_ext[layer, 3 + r]
        for d in range(-3, 4):
            y = x if d == 0 else pltpu.roll(x, (COLS - d) % COLS, axis=1)
            shifted[:, d + 3, 3 + r] = y.reshape(GROUPS, 16, COLS)

    def conv_own(layer, g):
        x = jnp.concatenate(
            [shifted[g, :, 0:16].reshape(7 * 256, COLS), shifted[g, :, 8:24].reshape(7 * 256, COLS)], axis=1
        )
        got = jnp.dot(conv_w[layer, g], x, preferred_element_type=F32)
        for k in range(2):
            mixed[8 * k : 8 * k + 8, g] = got[:, k * COLS : (k + 1) * COLS].reshape(8, 16, COLS)

    def halo_rows(layer, upper):
        some = lane[0:16]
        for g in range(GROUPS):
            at = slice(16 * g, 16 * g + 16)
            q = q_halo[layer, at].astype(F32)
            total = [jnp.zeros((16, COLS), F32)] * 3
            x, z = [], []
            for k in range(3):
                x.append(x_ext[layer, (19 if upper else 0) + k, at].astype(F32))
                z.append(pltpu.roll(q, 2 * COLS - 3 - 8 * (k if upper else 13 + k), axis=1))
            for d in range(7):
                by = d - 3
                for k in range(3):
                    if by == 0:
                        y = x[k]
                    else:
                        outside = some < by if by > 0 else some >= COLS + by
                        y = pltpu.roll(jnp.where(outside, z[k], x[k]), (COLS - by) % COLS, axis=1)
                    for r in range(3):
                        a = 6 + k - r if upper else k - r
                        if 0 <= a < 7:
                            total[r] = total[r] + tap_w[layer, a * 7 + d, at] * y
            for r in range(3):
                mixed[(13 if upper else 0) + r, g] += total[r]

    def fill_edge(layer):
        delta = q_mid[layer].astype(F32) - pack[layer].astype(F32)
        parts = [jnp.zeros((C, COLS), F32) for _ in SIDE]
        for a in range(7):
            by = 8 * (a - 3)
            if by > 0:
                rows = jnp.where(lane < by, 0.0, delta)
            elif by < 0:
                rows = jnp.where(lane >= COLS + by, 0.0, delta)
            else:
                rows = delta
            for k, d in enumerate(SIDE):
                parts[k] += tap_w[layer, a * 7 + d] * pltpu.roll(rows, (3 * COLS - by - (d - 3)) % COLS, axis=1)
        to = lane % 8
        total = jnp.zeros((C, COLS), F32)
        for part, d in zip(parts, SIDE):
            start = to + d - 3
            if d > 3:
                reach = (to < 3) & (start >= 3) & (start < 6)
            else:
                reach = (to >= 3) & (to < 6) & (start >= 0) & (start < 3)
            total = total + jnp.where(reach, part, 0.0)
        edge[...] = total

    def mlp(layer, at_rows):
        count = len(at_rows)

        def each(pick):
            return jnp.concatenate([pick(r) for r in at_rows], axis=1)

        def same(v):
            return jnp.concatenate([v] * count, axis=1)

        def mixed_row(r):
            beside = pltpu.roll(edge[...], (2 * COLS - 3 - 8 * r) % COLS, axis=1)
            return mixed[r].reshape(C, COLS) + jnp.where((lane < 3) | (lane >= COLS - 3), beside, 0.0)

        c = each(mixed_row) + same(colv[layer, 0])
        mean = jnp.sum(c, axis=0, keepdims=True) * (1.0 / C)
        c = c - mean
        var = jnp.sum(c * c, axis=0, keepdims=True) * (1.0 / C)
        n = c * lax.rsqrt(var + 1e-6) * same(colv[layer, 1]) + same(colv[layer, 2])
        ones = jnp.where(ids((32, count * COLS), 0) < 2, 1.0, 0.0)
        n = jnp.concatenate([n, ones], axis=0).astype(BF)
        half = jnp.dot(w_e[layer], n, preferred_element_type=F32)
        h = (half + half * lax.erf(half * np.float32(np.sqrt(2.0)))).astype(BF)
        u = jnp.dot(w_r[layer], h, preferred_element_type=F32) + same(colv[layer, 3])
        x = each(lambda r: x_ext[layer, 3 + r]).astype(F32)
        flags = each(lambda r: mask[r : r + 1, :]).astype(F32)
        y = flags * (x + u)
        for k, r in enumerate(at_rows):
            part = y[:, k * COLS : (k + 1) * COLS]
            if layer == LAYERS - 1:
                cells[pl.ds(r, C, stride=ROWS), :] = part
            else:
                x_ext[layer + 1, 3 + r] = part.astype(BF)

    loads[0].wait()
    cells[...] = raw[...].astype(F32).reshape(C * ROWS, COLS)

    def take_rows(rows):
        for r in rows:
            x_ext[0, 3 + r] = cells[pl.ds(r, C, stride=ROWS), :].astype(BF)

    take_rows((0, 1, 2, 13, 14, 15))
    fill_mirror(0)
    take_rows(range(3, 13))
    add_pack(0, range(ROWS), fresh=True)
    pl.semaphore_wait(barrier, n_peers)
    send_pack(0)
    send_high(0)
    send_low(0)
    send_corners(0)
    for rows in (slice(0, 3), slice(19, 24)):
        shifted[:, :, rows] = jnp.zeros((GROUPS, 7, rows.stop - rows.start, 16, COLS), BF)
    for one in loads[1:]:
        one.wait()
    build_weights(0)

    def interior(layer):
        for r in range(3, 13, 2):
            mlp(layer, (r, r + 1))

    for layer in range(LAYERS):
        onward = layer + 1 < LAYERS
        loop(ROWS, lambda r: shift_own(layer, r), ROWS)
        loop(GROUPS, lambda g: conv_own(layer, g), GROUPS)
        take_pack(layer)
        fill_edge(layer)
        interior(layer)
        if onward:
            add_pack(layer + 1, range(3, 13), fresh=True)
        take_corners(layer)
        take_low(layer)
        take_high(layer)
        halo_rows(layer, False)
        halo_rows(layer, True)
        mlp(layer, (0, 1, 2))
        mlp(layer, (13, 14, 15))
        if onward:
            add_pack(layer + 1, (0, 1, 2, 13, 14, 15))
            send_pack(layer + 1)
            fill_mirror(layer + 1)
            send_high(layer + 1)
            send_low(layer + 1)
            send_corners(layer + 1)
            build_weights(layer + 1)
    out[...] = cells[...].reshape(C, ROWS, COLS).astype(BF)
    for layer in range(LAYERS):
        wait_sends(layer)


def per_device(
    field, land_mask, depth_kernel, depth_bias, norm_gain, norm_bias, w_expand, b_expand, w_reduce, b_reduce
):
    taps = jnp.transpose(depth_kernel, (2, 3, 0, 1)).reshape(49, LAYERS, C)
    args = (
        field, land_mask, taps, depth_bias, norm_gain, norm_bias, jnp.transpose(w_expand, (0, 2, 1)), b_expand,
        w_reduce, b_reduce,
    )
    tile = (LAYERS, C, COLS)
    held = [pltpu.VMEM(a.shape, a.dtype) for a in args]
    scratch = held + [
        pltpu.VMEM((C * ROWS, COLS), F32),
        pltpu.VMEM((LAYERS, ROWS + 6, C, COLS), BF),
    ]
    scratch += [pltpu.VMEM(tile, BF)] * 5
    scratch += [
        pltpu.VMEM((LAYERS, 3, C, COLS), BF),
        pltpu.VMEM((LAYERS, COLS, COLS), BF),
        pltpu.VMEM((LAYERS, 32, COLS), BF),
        pltpu.VMEM((LAYERS, 2, COLS, COLS), BF),
        pltpu.VMEM((COLS, COLS), F32),
        pltpu.VMEM((LAYERS, HID, COLS), BF),
        pltpu.VMEM((LAYERS, GROUPS, COLS, 7 * 256), BF),
        pltpu.VMEM((LAYERS, 49, C, COLS), F32),
        pltpu.VMEM((LAYERS, 4, C, COLS), F32),
        pltpu.VMEM((GROUPS, 7, ROWS + 8, 16, COLS), BF),
        pltpu.VMEM((ROWS, GROUPS, 16, COLS), F32),
        pltpu.VMEM((C, COLS), F32),
        pltpu.SemaphoreType.DMA((len(args),)),
        pltpu.SemaphoreType.DMA((11 * LAYERS,)),
        pltpu.SemaphoreType.DMA((11 * LAYERS,)),
    ]
    return pl.pallas_call(
        kernel,
        out_shape=jax.ShapeDtypeStruct((C, ROWS, COLS), BF),
        in_specs=[pl.BlockSpec(memory_space=pltpu.HBM)] * len(args),
        out_specs=pl.BlockSpec(memory_space=pltpu.VMEM),
        scratch_shapes=scratch,
        compiler_params=pltpu.CompilerParams(
            collective_id=0, has_side_effects=True, vmem_limit_bytes=40 * 1024 * 1024
        ),
    )(*[pltpu.with_memory_space_constraint(a, pltpu.HBM) for a in args])


def solution(mesh):
    placed = (P(None, "lat", "lon"), P("lat", "lon"), P(), P(), P(), P(), P(), P(), P(), P())
    return jax.shard_map(
        per_device, mesh=mesh, in_specs=placed, out_specs=P(None, "lat", "lon"), check_vma=False
    )
```
